256 devices in a mesh: dp: 2 (over x_hi), tensor: 8 (over y, core), context: 16 (over x_lo, z).
Axes of the slice: x: 4 (x_hi: 2, x_lo: 2; x = x_hi * 2 + x_lo), y: 4, z: 8, core: 2. Of those that a mesh axis runs over, the one named last changes fastest.
Arguments:
- gate_out: bfloat16 [4096, 8192], P(('dp', 'context'), 'tensor'), parts along dimension 0, may hold values from -6 to 6
- gate_in: bfloat16 [4096, 8192], P(('dp', 'context'), 'tensor'), parts along dimension 0, may hold values from -6 to 6
- values_in: bfloat16 [4096, 8192], P(('dp', 'context'), 'tensor'), parts along dimension 0, may hold values from -6 to 6
- long_filter: bfloat16 [2048, 8192], P('context', 'tensor'), may hold values from -0.125 to 0.125
- skip_gain: float32 [8192], P('tensor'), may hold values from 0.25 to 2
- grad_out: bfloat16 [4096, 8192], P(('dp', 'context'), 'tensor'), parts along dimension 0, may hold values from -6 to 6
Outputs:
- grad_gate_out: bfloat16 [4096, 8192], P(('dp', 'context'), 'tensor'), parts along dimension 0
- grad_gate_in: bfloat16 [4096, 8192], P(('dp', 'context'), 'tensor'), parts along dimension 0
- grad_values: bfloat16 [4096, 8192], P(('dp', 'context'), 'tensor'), parts along dimension 0
- grad_filter: float32 [4096, 8192], P(('dp', 'context'), 'tensor'), parts along dimension 0
The draws below stay inside these ranges and needn't reach their ends.
There are 2 independent parts, one for each index of `dp`. The reference program is written for one: setup_inputs(seed, part) draws one part's arguments, and reference() takes and returns one part's arrays. A program takes and returns all parts, laid end to end along the dimension named above; an argument that names none is the same for every part. Nothing has to cross between parts.
All inputs are finite; a program needn't handle non-finite values.
Results may differ from the reference program's by a relative error of at most 0.0013.
Values sent between devices are 32-bit elements; how exact they have to be, the bound alone decides.
No kernel may reach another device: no remote copies, remote signals or barrier semaphores. Data moves between devices by JAX's collectives and lax.ppermute only.
A program may use at most 64 MiB of HBM per device.

```python
import math
import jax
import jax.numpy as jnp

D = 8192
SEQ = 2048


def steps_of(stream_key, extent, cuts, low, largest):
    factor_of = 1.0
    for dim, blocks in cuts:
        draws = jax.random.uniform(jax.random.fold_in(jax.random.fold_in(stream_key, 6), dim), (blocks,), jnp.float32, low / len(cuts), largest / len(cuts))
        factor_of = factor_of * jnp.repeat(jnp.exp(draws), extent[dim] // blocks).reshape((-1,) + (1,) * (len(extent) - 1 - dim))
    return factor_of


def noise(own_key, extent, deviation, limit, cuts=(), held_as=jnp.bfloat16):
    loudness = steps_of(own_key, extent, cuts, -0.22, 0.18) if cuts else 1.0
    result = jax.random.normal(own_key, extent, jnp.float32) * deviation * loudness
    return jnp.minimum(jnp.maximum(result, -limit), limit).astype(held_as)


def setup_inputs(seed: int = 0, part: int = 0) -> dict:
    seeds = jax.random.split(jax.random.key(seed), 7)
    own_keys = jax.random.split(jax.random.fold_in(seeds[6], part), 7)
    return {
        "gate_out": noise(own_keys[0], (SEQ, D), 1.0, 6.0, ((0, 16), (1, 8))),
        "gate_in": noise(own_keys[1], (SEQ, D), 1.0, 6.0, ((0, 16), (1, 8))),
        "values_in": noise(own_keys[2], (SEQ, D), 1.0, 6.0, ((0, 16), (1, 8))),
        "long_filter": noise(seeds[3], (SEQ, D), SEQ ** -0.5, 0.125, ((0, 16), (1, 8))),
        "skip_gain": jnp.clip(0.25 + 1.75 * jax.random.uniform(seeds[4], (D,), jnp.float32) ** steps_of(seeds[4], (D,), ((0, 8),), -0.2, 0.2), 0.25, 2.0),
        "grad_out": noise(own_keys[5], (SEQ, D), 1.0, 6.0, ((0, 16), (1, 8))),
    }


def channel_block(gate_out, gate_in, values_in, long_filter, skip_gain, grad_out):
    length = 2 * SEQ
    mixed_in = gate_in.astype(jnp.float32) * values_in.astype(jnp.float32)
    grad_mixed = grad_out.astype(jnp.float32) * gate_out.astype(jnp.float32)
    filt_spec = jnp.fft.rfft(long_filter.astype(jnp.float32), n=length, axis=0)
    mixed_spec = jnp.fft.rfft(mixed_in, n=length, axis=0)
    grad_spec = jnp.fft.rfft(grad_mixed, n=length, axis=0)
    conv_out = jnp.fft.irfft(filt_spec * mixed_spec, n=length, axis=0)[:SEQ]
    grad_mix = jnp.fft.irfft(jnp.conj(filt_spec) * grad_spec, n=length, axis=0)[:SEQ]
    lagged = jnp.fft.irfft(jnp.conj(mixed_spec) * grad_spec, n=length, axis=0)[:SEQ]
    mixer_state = conv_out + skip_gain[None, :] * mixed_in
    grad_mix = grad_mix + skip_gain[None, :] * grad_mixed
    grad_gate_out = (grad_out.astype(jnp.float32) * mixer_state).astype(jnp.bfloat16)
    grad_gate_in = (grad_mix * values_in.astype(jnp.float32)).astype(jnp.bfloat16)
    grad_values = (grad_mix * gate_in.astype(jnp.float32)).astype(jnp.bfloat16)
    grad_filter = (lagged * (1.0 / math.sqrt(SEQ))).astype(jnp.float32)
    return (grad_gate_out, grad_gate_in, grad_values, grad_filter)

def reference(gate_out, gate_in, values_in, long_filter, skip_gain, grad_out):
    block_width = min(D, 1024)
    pieces = []
    for block_start in range(0, D, block_width):
        stop = block_start + block_width
        pieces.append(channel_block(gate_out[:, block_start:stop], gate_in[:, block_start:stop], values_in[:, block_start:stop], long_filter[:, block_start:stop], skip_gain[block_start:stop], grad_out[:, block_start:stop]))
    return (jnp.concatenate([piece[0] for piece in pieces], axis=1), jnp.concatenate([piece[1] for piece in pieces], axis=1), jnp.concatenate([piece[2] for piece in pieces], axis=1), jnp.concatenate([piece[3] for piece in pieces], axis=1))
```

```python
import math

import jax
import jax.numpy as jnp
import numpy as np
from jax import lax
from jax.experimental import pallas as pl
from jax.experimental.pallas import tpu as pltpu
from jax.sharding import PartitionSpec as P

LANES = 128
SIGNALS = 3


def complex_add(a, b):
    return (a[0] + b[0], a[1] + b[1])


def complex_sub(a, b):
    return (a[0] - b[0], a[1] - b[1])


def rotate(a, angle_num, angle_den):
    num = angle_num % angle_den
    re, im = a
    if num == 0:
        return a
    if 4 * num == angle_den:
        return (-im, re)
    if 2 * num == angle_den:
        return (-re, -im)
    if 4 * num == 3 * angle_den:
        return (im, -re)
    if (8 * num) % angle_den == 0:
        half = math.sqrt(0.5)
        octant = (8 * num) // angle_den
        if octant == 1:
            return ((re - im) * half, (re + im) * half)
        if octant == 3:
            return ((re + im) * -half, (re - im) * half)
        if octant == 5:
            return ((im - re) * half, (re + im) * -half)
        return ((re + im) * half, (im - re) * half)
    c = math.cos(2.0 * math.pi * num / angle_den)
    s = math.sin(2.0 * math.pi * num / angle_den)
    return (re * c - im * s, re * s + im * c)


def complex_fft(values, sign):
    n = len(values)
    if n == 1:
        return values
    half = n // 2
    sums = [complex_add(values[p], values[p + half]) for p in range(half)]
    diffs = [complex_sub(values[p], values[p + half]) for p in range(half)]
    diffs = [rotate(d, sign * p, n) for p, d in enumerate(diffs)]
    even = complex_fft(sums, sign)
    odd = complex_fft(diffs, sign)
    return [v for pair in zip(even, odd) for v in pair]


def odd_forward(diffs, n, out):
    quarter = n // 4
    if n == 2:
        out[1] = (diffs[0], None)
        return
    twisted = [rotate((diffs[p], -diffs[p + quarter]), -p, n) for p in range(quarter)]
    for r, value in enumerate(complex_fft(twisted, -1)):
        k = 4 * r + 1
        if 2 * k < n:
            out[k] = value
        else:
            out[n - k] = (value[0], -value[1])


def real_forward(values, n):
    out = {}
    half = n // 2
    if len(values) == half:
        sums, diffs = values, values
    else:
        sums = [values[p] + values[p + half] for p in range(half)]
        diffs = [values[p] - values[p + half] for p in range(half)]
    if half == 1:
        out[0] = (sums[0], None)
    else:
        for k, value in real_forward(sums, half).items():
            out[2 * k] = value
    odd_forward(diffs, n, out)
    return out


def real_inverse(spec, n, first_half):
    half, quarter = n // 2, n // 4
    if n == 2:
        return [spec[0][0] + spec[1][0], spec[0][0] - spec[1][0]]
    evens = real_inverse({k // 2: v for k, v in spec.items() if k % 2 == 0}, half, False)
    odds = []
    for r in range(quarter):
        k = 4 * r + 1
        odds.append(spec[k] if 2 * k < n else (spec[n - k][0], -spec[n - k][1]))
    turned = [rotate(v, p, n) for p, v in enumerate(complex_fft(odds, 1))]
    odd_part = [v[0] for v in turned] + [-v[1] for v in turned]
    front = [evens[p] + odd_part[p] for p in range(half)]
    if first_half:
        return front
    return front + [evens[p] - odd_part[p] for p in range(half)]


def table(blocks):
    rows_all = 2 * blocks
    length = rows_all * LANES
    lane = np.arange(LANES)
    out = []
    for k1 in range(blocks + 1):
        angles = 2.0 * np.pi * (lane[:, None] * (k1 + rows_all * lane[None, :]) % length) / length
        cosine, sine = np.cos(angles), np.sin(angles)
        out.append(np.block([[cosine, -sine], [sine, cosine]]))
    whole = np.stack(out).astype(np.float32)
    high = whole.astype(jnp.bfloat16)
    low = (whole - high.astype(np.float32)).astype(jnp.bfloat16)
    return high, low


def split(value):
    high = value.astype(jnp.bfloat16)
    return high, (value - high.astype(jnp.float32)).astype(jnp.bfloat16)


def dot_parts(left, right_high, right_low, right_dim):
    dims = (((1,), (right_dim,)), ((), ()))
    high, low = split(left)
    total = lax.dot_general(low, right_high, dims, preferred_element_type=jnp.float32)
    total += lax.dot_general(high, right_low, dims, preferred_element_type=jnp.float32)
    return total + lax.dot_general(high, right_high, dims, preferred_element_type=jnp.float32)


def pack_kernel(gate_in, values_in, long_filter, grad_out, gate_out, packed):
    share = packed.shape[1] // SIGNALS
    mixed = gate_in[...].astype(jnp.float32) * values_in[...].astype(jnp.float32)
    grad = grad_out[...].astype(jnp.float32) * gate_out[...].astype(jnp.float32)
    for s, value in enumerate((mixed, long_filter[...].astype(jnp.float32), grad)):
        turned = value.T
        for b in range(packed.shape[0]):
            packed[b, s * share:(s + 1) * share, :] = turned[b * share:(b + 1) * share]


def convolve_kernel(received, high, low, result, spectrum, inverted):
    blocks, rows, _ = received.shape
    share = rows // SIGNALS
    rows_all = 2 * blocks
    scale = 2.0 / (rows_all * LANES)

    def forward(tile, carry):
        at = pl.ds(pl.multiple_of(tile * 8, 8), 8)
        out = real_forward([received[p, at, :] for p in range(blocks)], rows_all)
        for k1 in range(blocks + 1):
            re, im = out[k1]
            spectrum[k1, at, :LANES] = re
            spectrum[k1, at, LANES:] = jnp.zeros_like(re) if im is None else im
        return carry

    lax.fori_loop(0, rows // 8, forward, 0)

    for k1 in range(blocks + 1):
        freq = dot_parts(spectrum[k1], high[k1], low[k1], 0)
        mixed_re, mixed_im = freq[:share, :LANES], freq[:share, LANES:]
        filt_re, filt_im = freq[share:2 * share, :LANES], freq[share:2 * share, LANES:]
        grad_re, grad_im = freq[2 * share:, :LANES], freq[2 * share:, LANES:]
        factor = scale * 0.5 if k1 in (0, blocks) else scale
        grad_re, grad_im = grad_re * factor, grad_im * factor
        filt_scaled_re, filt_scaled_im = filt_re * factor, filt_im * factor
        conv = jnp.concatenate([
            filt_scaled_re * mixed_re - filt_scaled_im * mixed_im,
            filt_scaled_re * mixed_im + filt_scaled_im * mixed_re], axis=1)
        back = jnp.concatenate([
            filt_re * grad_re + filt_im * grad_im, filt_re * grad_im - filt_im * grad_re], axis=1)
        lag = jnp.concatenate([
            mixed_re * grad_re + mixed_im * grad_im, mixed_re * grad_im - mixed_im * grad_re], axis=1)
        products = jnp.concatenate([conv, back, lag], axis=0)
        inverted[k1] = dot_parts(products, high[k1], low[k1], 1)

    def backward(tile, carry):
        at = pl.ds(pl.multiple_of(tile * 8, 8), 8)
        spec = {k1: (inverted[k1, at, :LANES], inverted[k1, at, LANES:]) for k1 in range(blocks + 1)}
        for p, value in enumerate(real_inverse(spec, rows_all, True)):
            result[p, at, :] = value
        return carry

    lax.fori_loop(0, rows // 8, backward, 0)


def unpack_kernel(seq_len, returned, gate_in, values_in, skip_gain, grad_out, gate_out,
                  grad_gate_out, grad_gate_in, grad_values, grad_filter):
    share = returned.shape[1] // SIGNALS
    values, gate = values_in[...].astype(jnp.float32), gate_in[...].astype(jnp.float32)
    cotangent = grad_out[...].astype(jnp.float32)
    skip = skip_gain[...]

    def turned(s):
        return jnp.concatenate(
            [returned[b, s * share:(s + 1) * share, :] for b in range(returned.shape[0])], axis=0).T

    mixer_state = turned(0) + skip * (gate * values)
    grad_gate_out[...] = (cotangent * mixer_state).astype(jnp.bfloat16)
    grad_mix = turned(1) + skip * (cotangent * gate_out[...].astype(jnp.float32))
    grad_gate_in[...] = (grad_mix * values).astype(jnp.bfloat16)
    grad_values[...] = (grad_mix * gate).astype(jnp.bfloat16)
    grad_filter[...] = turned(2) * (1.0 / math.sqrt(seq_len))


def local(gate_out, gate_in, values_in, long_filter, skip_gain, grad_out):
    tokens, channels = gate_out.shape
    devices = lax.axis_size("context")
    seq_len = tokens * devices
    share = channels // devices
    rows = SIGNALS * share
    group = LANES // share
    steps = channels // LANES
    high, low = table(devices)

    def plain(columns_dim=1):
        return pl.BlockSpec((tokens, LANES), lambda i: (0, i))

    packed_spec = pl.BlockSpec((group, rows, tokens), lambda i: (i, 0, 0))
    packed = pl.pallas_call(
        pack_kernel,
        grid=(steps,),
        in_specs=[plain()] * 5,
        out_specs=packed_spec,
        out_shape=jax.ShapeDtypeStruct((devices, rows, tokens), jnp.float32),
        name="pack",
    )(gate_in, values_in, long_filter, grad_out, gate_out)
    received = lax.all_to_all(packed, "context", split_axis=0, concat_axis=0, tiled=True)
    result = pl.pallas_call(
        convolve_kernel,
        out_shape=jax.ShapeDtypeStruct((devices, rows, tokens), jnp.float32),
        in_specs=[pl.BlockSpec(memory_space=pltpu.VMEM)] * 3,
        out_specs=pl.BlockSpec(memory_space=pltpu.VMEM),
        scratch_shapes=[pltpu.VMEM((devices + 1, rows, 2 * LANES), jnp.float32)] * 2,
        compiler_params=pltpu.CompilerParams(vmem_limit_bytes=40 * 1024 * 1024),
        name="convolve",
    )(received, jnp.asarray(high), jnp.asarray(low))
    returned = lax.all_to_all(result, "context", split_axis=0, concat_axis=0, tiled=True)
    wide = [jax.ShapeDtypeStruct((tokens, channels), jnp.bfloat16)] * 3
    return tuple(pl.pallas_call(
        lambda *refs: unpack_kernel(seq_len, *refs),
        grid=(steps,),
        in_specs=[packed_spec, plain(), plain(), pl.BlockSpec((1, LANES), lambda i: (0, i)), plain(), plain()],
        out_specs=[plain()] * 4,
        out_shape=wide + [jax.ShapeDtypeStruct((tokens, channels), jnp.float32)],
        name="unpack",
    )(returned, gate_in, values_in, skip_gain[None, :], grad_out, gate_out))


def solution(mesh):
    sequence = P(("dp", "context"), "tensor")
    return jax.shard_map(
        local,
        mesh=mesh,
        in_specs=(sequence, sequence, sequence, P("context", "tensor"), P("tensor"), sequence),
        out_specs=(sequence,) * 4,
        check_vma=False,
    )
```

```python
import math

import jax
import jax.numpy as jnp
import numpy as np
from jax import lax
from jax.experimental import pallas as pl
from jax.experimental.pallas import tpu as pltpu
from jax.sharding import PartitionSpec as P

LANES = 128
AXES = ("line", "dp", "column")


def complex_add(a, b):
    return (a[0] + b[0], a[1] + b[1])


def complex_sub(a, b):
    return (a[0] - b[0], a[1] - b[1])


def rotate(a, angle_num, angle_den):
    num = angle_num % angle_den
    re, im = a
    if num == 0:
        return a
    if 4 * num == angle_den:
        return (-im, re)
    if 2 * num == angle_den:
        return (-re, -im)
    if 4 * num == 3 * angle_den:
        return (im, -re)
    if (8 * num) % angle_den == 0:
        half = math.sqrt(0.5)
        octant = (8 * num) // angle_den
        if octant == 1:
            return ((re - im) * half, (re + im) * half)
        if octant == 3:
            return ((re + im) * -half, (re - im) * half)
        if octant == 5:
            return ((im - re) * half, (re + im) * -half)
        return ((re + im) * half, (im - re) * half)
    c = math.cos(2.0 * math.pi * num / angle_den)
    s = math.sin(2.0 * math.pi * num / angle_den)
    return (re * c - im * s, re * s + im * c)


def complex_fft(values, sign):
    n = len(values)
    if n == 1:
        return values
    half = n // 2
    sums = [complex_add(values[p], values[p + half]) for p in range(half)]
    diffs = [complex_sub(values[p], values[p + half]) for p in range(half)]
    diffs = [rotate(d, sign * p, n) for p, d in enumerate(diffs)]
    even = complex_fft(sums, sign)
    odd = complex_fft(diffs, sign)
    return [v for pair in zip(even, odd) for v in pair]


def odd_forward(diffs, n, out):
    quarter = n // 4
    if n == 2:
        out[1] = (diffs[0], None)
        return
    twisted = [rotate((diffs[p], -diffs[p + quarter]), -p, n) for p in range(quarter)]
    for r, value in enumerate(complex_fft(twisted, -1)):
        k = 4 * r + 1
        if 2 * k < n:
            out[k] = value
        else:
            out[n - k] = (value[0], -value[1])


def real_forward(values, n):
    out = {}
    half = n // 2
    if len(values) == half:
        sums, diffs = values, values
    else:
        sums = [values[p] + values[p + half] for p in range(half)]
        diffs = [values[p] - values[p + half] for p in range(half)]
    if half == 1:
        out[0] = (sums[0], None)
    else:
        for k, value in real_forward(sums, half).items():
            out[2 * k] = value
    odd_forward(diffs, n, out)
    return out


def real_inverse(spec, n, first_half):
    half, quarter = n // 2, n // 4
    if n == 2:
        return [spec[0][0] + spec[1][0], spec[0][0] - spec[1][0]]
    evens = real_inverse({k // 2: v for k, v in spec.items() if k % 2 == 0}, half, False)
    odds = []
    for r in range(quarter):
        k = 4 * r + 1
        odds.append(spec[k] if 2 * k < n else (spec[n - k][0], -spec[n - k][1]))
    turned = [rotate(v, p, n) for p, v in enumerate(complex_fft(odds, 1))]
    odd_part = [v[0] for v in turned] + [-v[1] for v in turned]
    front = [evens[p] + odd_part[p] for p in range(half)]
    if first_half:
        return front
    return front + [evens[p] - odd_part[p] for p in range(half)]


def table(blocks):
    rows_all = 2 * blocks
    length = rows_all * LANES
    lane = np.arange(LANES)
    out = []
    for k1 in range(blocks + 1):
        angles = 2.0 * np.pi * (lane[:, None] * (k1 + rows_all * lane[None, :]) % length) / length
        cosine, sine = np.cos(angles), np.sin(angles)
        out.append(np.block([[cosine, -sine], [sine, cosine]]))
    whole = np.stack(out).astype(np.float32)
    high = whole.astype(jnp.bfloat16)
    low = (whole - high.astype(np.float32)).astype(jnp.bfloat16)
    return high, low


def split(value):
    high = value.astype(jnp.bfloat16)
    return high, (value - high.astype(jnp.float32)).astype(jnp.bfloat16)


def dot_parts(left, right_high, right_low, right_dim):
    dims = (((1,), (right_dim,)), ((), ()))
    high, low = split(left)
    total = lax.dot_general(low, right_high, dims, preferred_element_type=jnp.float32)
    total += lax.dot_general(high, right_low, dims, preferred_element_type=jnp.float32)
    return total + lax.dot_general(high, right_high, dims, preferred_element_type=jnp.float32)


def pack_kernel(gate_in, values_in, long_filter, grad_out, gate_out, packed):
    share = channels_of(packed.shape[1], 1 + 1 + 0.5)
    mixed = gate_in[...].astype(jnp.float32) * values_in[...].astype(jnp.float32)
    grad = grad_out[...].astype(jnp.float32) * gate_out[...].astype(jnp.float32)
    filt = long_filter[...].astype(jnp.float32)
    half = share // 2
    second = lax.axis_index("dp") == 1
    for lane in range(0, mixed.shape[1], LANES):
        at = slice(lane, lane + LANES)
        mixed_t, grad_t, filt_t = mixed[:, at].T, grad[:, at].T, filt[:, at].T
        for b in range(LANES // share):
            to, row = lane // share + b, b * share
            packed[to, :share, :] = mixed_t[row:row + share]
            packed[to, share:2 * share, :] = grad_t[row:row + share]
            packed[to, 2 * share:, :] = jnp.where(
                second, filt_t[row + half:row + share], filt_t[row:row + half])


def channels_of(rows, signals):
    return int(rows / signals)


def convolve_kernel(shape, received, high, low, result, spectrum, inverted):
    lines, parts, columns = shape
    blocks = lines * columns
    share = result.shape[1] // 3
    half = share // 2
    rows_all = 2 * blocks
    scale = 2.0 / (rows_all * LANES)
    grad_row, filt_row = parts * share, 2 * parts * share

    def source(line, part, column):
        return (line * parts + part) * columns + column

    def forward(part, taken, given):
        out = real_forward(
            [received[source(x, part, z), pl.ds(taken, 8), :] for x in range(lines) for z in range(columns)],
            rows_all)
        for k1 in range(blocks + 1):
            re, im = out[k1]
            spectrum[k1, pl.ds(given, 8), :LANES] = re
            spectrum[k1, pl.ds(given, 8), LANES:] = jnp.zeros_like(re) if im is None else im

    for part in range(parts):
        def tile_of_signals(tile, carry):
            start = pl.multiple_of(tile * 8, 8)
            forward(part, start, pl.multiple_of(part * share + start, 8))
            forward(part, pl.multiple_of(share + start, 8), pl.multiple_of(grad_row + part * share + start, 8))
            return carry

        lax.fori_loop(0, share // 8, tile_of_signals, 0)

        def tile_of_filter(tile, carry):
            start = pl.multiple_of(tile * 8, 8)
            forward(part, pl.multiple_of(2 * share + start, 8), pl.multiple_of(filt_row + part * half + start, 8))
            return carry

        lax.fori_loop(0, half // 8, tile_of_filter, 0)

    for k1 in range(blocks + 1):
        freq = dot_parts(spectrum[k1], high[k1], low[k1], 0)
        factor = scale * 0.5 if k1 in (0, blocks) else scale
        filt_re, filt_im = freq[filt_row:, :LANES], freq[filt_row:, LANES:]
        filt_re, filt_im = filt_re * factor, filt_im * factor
        products = []
        for part in range(parts):
            mixed = slice(part * share, (part + 1) * share)
            grad = slice(grad_row + part * share, grad_row + (part + 1) * share)
            mixed_re, mixed_im = freq[mixed, :LANES], freq[mixed, LANES:]
            grad_re, grad_im = freq[grad, :LANES], freq[grad, LANES:]
            products.append(jnp.concatenate([
                filt_re * mixed_re - filt_im * mixed_im, filt_re * mixed_im + filt_im * mixed_re], axis=1))
            products.append(jnp.concatenate([
                filt_re * grad_re + filt_im * grad_im, filt_re * grad_im - filt_im * grad_re], axis=1))
            mixed_re, mixed_im = mixed_re * factor, mixed_im * factor
            products.append(jnp.concatenate([
                mixed_re * grad_re + mixed_im * grad_im, mixed_re * grad_im - mixed_im * grad_re], axis=1))
        inverted[k1] = dot_parts(jnp.concatenate(products, axis=0), high[k1], low[k1], 1)

    for part in range(parts):
        def backward(tile, carry):
            start = pl.multiple_of(tile * 8, 8)
            at = pl.ds(pl.multiple_of(part * 3 * share + start, 8), 8)
            spec = {k1: (inverted[k1, at, :LANES], inverted[k1, at, LANES:]) for k1 in range(blocks + 1)}
            values = real_inverse(spec, rows_all, True)
            for x in range(lines):
                for z in range(columns):
                    result[source(x, part, z), pl.ds(start, 8), :] = values[x * columns + z]
            return carry

        lax.fori_loop(0, 3 * share // 8, backward, 0)


def unpack_kernel(seq_len, returned, gate_in, values_in, skip_gain, grad_out, gate_out,
                  grad_gate_out, grad_gate_in, grad_values, grad_filter):
    share = returned.shape[1] // 3
    for lane in range(0, gate_in.shape[1], LANES):
        at = slice(lane, lane + LANES)
        values, gate = values_in[:, at].astype(jnp.float32), gate_in[:, at].astype(jnp.float32)
        cotangent = grad_out[:, at].astype(jnp.float32)
        skip = skip_gain[:, at]

        def turned(s):
            return jnp.concatenate(
                [returned[lane // share + b, s * share:(s + 1) * share, :] for b in range(LANES // share)],
                axis=0).T

        mixer_state = turned(0) + skip * (gate * values)
        grad_gate_out[:, at] = (cotangent * mixer_state).astype(jnp.bfloat16)
        grad_mix = turned(1) + skip * (cotangent * gate_out[:, at].astype(jnp.float32))
        grad_gate_in[:, at] = (grad_mix * values).astype(jnp.bfloat16)
        grad_values[:, at] = (grad_mix * gate).astype(jnp.bfloat16)
        grad_filter[:, at] = turned(2) * (1.0 / math.sqrt(seq_len))


def pack(width, devices, gate_in, values_in, long_filter, grad_out, gate_out):
    tokens, channels = gate_in.shape
    share = channels // devices
    rows = 2 * share + share // 2
    plain = pl.BlockSpec((tokens, width), lambda i: (0, i))
    return pl.pallas_call(
        pack_kernel,
        grid=(channels // width,),
        in_specs=[plain] * 5,
        out_specs=pl.BlockSpec((width // share, rows, tokens), lambda i: (i, 0, 0)),
        out_shape=jax.ShapeDtypeStruct((devices, rows, tokens), jnp.float32),
        name="pack",
    )(gate_in, values_in, long_filter, grad_out, gate_out)


def convolve(shape, received, high, low):
    devices, rows, tokens = received.shape
    share = channels_of(rows, 2.5)
    blocks = shape[0] * shape[2]
    forward_rows = (2 * shape[1] + 1) * share
    inverse_rows = 3 * shape[1] * share
    return pl.pallas_call(
        lambda *refs: convolve_kernel(shape, *refs),
        out_shape=jax.ShapeDtypeStruct((devices, 3 * share, tokens), jnp.float32),
        in_specs=[pl.BlockSpec(memory_space=pltpu.VMEM)] * 3,
        out_specs=pl.BlockSpec(memory_space=pltpu.VMEM),
        scratch_shapes=[pltpu.VMEM((blocks + 1, forward_rows, 2 * LANES), jnp.float32),
                        pltpu.VMEM((blocks + 1, inverse_rows, 2 * LANES), jnp.float32)],
        compiler_params=pltpu.CompilerParams(vmem_limit_bytes=40 * 1024 * 1024),
        name="convolve",
    )(received, high, low)


def unpack(width, seq_len, returned, gate_in, values_in, skip_gain, grad_out, gate_out):
    devices, rows, tokens = returned.shape
    channels = gate_in.shape[1]
    share = channels // devices
    plain = pl.BlockSpec((tokens, width), lambda i: (0, i))
    wide = [jax.ShapeDtypeStruct((tokens, channels), jnp.bfloat16)] * 3
    return tuple(pl.pallas_call(
        lambda *refs: unpack_kernel(seq_len, *refs),
        grid=(channels // width,),
        in_specs=[pl.BlockSpec((width // share, rows, tokens), lambda i: (i, 0, 0)), plain, plain,
                  pl.BlockSpec((1, width), lambda i: (0, i)), plain, plain],
        out_specs=[plain] * 4,
        out_shape=wide + [jax.ShapeDtypeStruct((tokens, channels), jnp.float32)],
        name="unpack",
    )(returned, gate_in, values_in, skip_gain[None, :], grad_out, gate_out))


PACK_WIDTH = 256
UNPACK_WIDTH = 256


def local(gate_out, gate_in, values_in, long_filter, skip_gain, grad_out):
    tokens = gate_out.shape[0]
    shape = tuple(lax.axis_size(axis) for axis in AXES)
    blocks = shape[0] * shape[2]
    high, low = (jnp.asarray(t) for t in table(blocks))
    packed = pack(PACK_WIDTH, math.prod(shape), gate_in, values_in, long_filter, grad_out, gate_out)
    received = lax.all_to_all(packed, AXES, split_axis=0, concat_axis=0, tiled=True)
    result = convolve(shape, received, high, low)
    returned = lax.all_to_all(result, AXES, split_axis=0, concat_axis=0, tiled=True)
    return unpack(UNPACK_WIDTH, tokens * blocks, returned, gate_in, values_in, skip_gain, grad_out, gate_out)


def solution(mesh):
    parts, tensor, context = mesh.devices.shape
    lines = 2
    mesh = jax.sharding.Mesh(
        mesh.devices.reshape(parts, tensor, lines, context // lines), ("dp", "tensor", "line", "column"))
    sequence = P(("dp", "line", "column"), "tensor")
    return jax.shard_map(
        local,
        mesh=mesh,
        in_specs=(sequence, sequence, sequence, P(("line", "column"), "tensor"), P("tensor"), sequence),
        out_specs=(sequence,) * 4,
        check_vma=False,
    )
```

```python
import math

import jax
import jax.numpy as jnp
import numpy as np
from jax import lax
from jax.experimental import pallas as pl
from jax.experimental.pallas import tpu as pltpu
from jax.sharding import PartitionSpec as P

LANES = 128


def complex_add(a, b):
    return (a[0] + b[0], a[1] + b[1])


def complex_sub(a, b):
    return (a[0] - b[0], a[1] - b[1])


def rotate(a, angle_num, angle_den):
    num = angle_num % angle_den
    re, im = a
    if num == 0:
        return a
    if 4 * num == angle_den:
        return (-im, re)
    if 2 * num == angle_den:
        return (-re, -im)
    if 4 * num == 3 * angle_den:
        return (im, -re)
    if (8 * num) % angle_den == 0:
        half = math.sqrt(0.5)
        octant = (8 * num) // angle_den
        if octant == 1:
            return ((re - im) * half, (re + im) * half)
        if octant == 3:
            return ((re + im) * -half, (re - im) * half)
        if octant == 5:
            return ((im - re) * half, (re + im) * -half)
        return ((re + im) * half, (im - re) * half)
    c = math.cos(2.0 * math.pi * num / angle_den)
    s = math.sin(2.0 * math.pi * num / angle_den)
    return (re * c - im * s, re * s + im * c)


def complex_fft(values, sign):
    n = len(values)
    if n == 1:
        return values
    half = n // 2
    sums = [complex_add(values[p], values[p + half]) for p in range(half)]
    diffs = [complex_sub(values[p], values[p + half]) for p in range(half)]
    diffs = [rotate(d, sign * p, n) for p, d in enumerate(diffs)]
    even = complex_fft(sums, sign)
    odd = complex_fft(diffs, sign)
    return [v for pair in zip(even, odd) for v in pair]


def odd_forward(diffs, n, out):
    quarter = n // 4
    if n == 2:
        out[1] = (diffs[0], None)
        return
    twisted = [rotate((diffs[p], -diffs[p + quarter]), -p, n) for p in range(quarter)]
    for r, value in enumerate(complex_fft(twisted, -1)):
        k = 4 * r + 1
        if 2 * k < n:
            out[k] = value
        else:
            out[n - k] = (value[0], -value[1])


def real_forward(values, n):
    out = {}
    half = n // 2
    if len(values) == half:
        sums, diffs = values, values
    else:
        sums = [values[p] + values[p + half] for p in range(half)]
        diffs = [values[p] - values[p + half] for p in range(half)]
    if half == 1:
        out[0] = (sums[0], None)
    else:
        for k, value in real_forward(sums, half).items():
            out[2 * k] = value
    odd_forward(diffs, n, out)
    return out


def real_inverse(spec, n, first_half):
    half, quarter = n // 2, n // 4
    if n == 2:
        return [spec[0][0] + spec[1][0], spec[0][0] - spec[1][0]]
    evens = real_inverse({k // 2: v for k, v in spec.items() if k % 2 == 0}, half, False)
    odds = []
    for r in range(quarter):
        k = 4 * r + 1
        odds.append(spec[k] if 2 * k < n else (spec[n - k][0], -spec[n - k][1]))
    turned = [rotate(v, p, n) for p, v in enumerate(complex_fft(odds, 1))]
    odd_part = [v[0] for v in turned] + [-v[1] for v in turned]
    front = [evens[p] + odd_part[p] for p in range(half)]
    if first_half:
        return front
    return front + [evens[p] - odd_part[p] for p in range(half)]


def table(blocks):
    rows_all = 2 * blocks
    length = rows_all * LANES
    lane = np.arange(LANES)
    out = []
    for k1 in range(blocks + 1):
        angles = 2.0 * np.pi * (lane[:, None] * (k1 + rows_all * lane[None, :]) % length) / length
        cosine, sine = np.cos(angles), np.sin(angles)
        out.append(np.block([[cosine, -sine], [sine, cosine]]))
    whole = np.stack(out).astype(np.float32)
    high = whole.astype(jnp.bfloat16)
    low = (whole - high.astype(np.float32)).astype(jnp.bfloat16)
    return high, low


def split(value):
    high = value.astype(jnp.bfloat16)
    return high, (value - high.astype(jnp.float32)).astype(jnp.bfloat16)


def dot_parts(left, right_high, right_low, right_dim):
    dims = (((1,), (right_dim,)), ((), ()))
    high, low = split(left)
    total = lax.dot_general(low, right_high, dims, preferred_element_type=jnp.float32)
    total += lax.dot_general(high, right_low, dims, preferred_element_type=jnp.float32)
    return total + lax.dot_general(high, right_high, dims, preferred_element_type=jnp.float32)


def pack_kernel(share, gate_in, values_in, long_filter, grad_out, gate_out, packed):
    mixed = gate_in[...].astype(jnp.float32) * values_in[...].astype(jnp.float32)
    grad = grad_out[...].astype(jnp.float32) * gate_out[...].astype(jnp.float32)
    filt = long_filter[...].astype(jnp.float32)
    for lane in range(0, mixed.shape[1], LANES):
        at = slice(lane, lane + LANES)
        mixed_t, grad_t, filt_t = mixed[:, at].T, grad[:, at].T, filt[:, at].T
        for b in range(LANES // share):
            to, row = lane // share + b, b * share
            packed[to, :share, :] = mixed_t[row:row + share]
            packed[to, share:2 * share, :] = filt_t[row:row + share]
            packed[to, 2 * share:, :] = grad_t[row:row + share]


def convolve_kernel(received, high, low, result, spectrum, inverted):
    blocks, rows, _ = received.shape
    share = rows // 3
    rows_all = 2 * blocks
    scale = 2.0 / (rows_all * LANES)

    def forward(tile, carry):
        at = pl.ds(pl.multiple_of(tile * 8, 8), 8)
        out = real_forward([received[p, at, :] for p in range(blocks)], rows_all)
        for k1 in range(blocks + 1):
            re, im = out[k1]
            spectrum[k1, at, :LANES] = re
            spectrum[k1, at, LANES:] = jnp.zeros_like(re) if im is None else im
        return carry

    lax.fori_loop(0, rows // 8, forward, 0)

    for k1 in range(blocks + 1):
        freq = dot_parts(spectrum[k1], high[k1], low[k1], 0)
        mixed_re, mixed_im = freq[:share, :LANES], freq[:share, LANES:]
        filt_re, filt_im = freq[share:2 * share, :LANES], freq[share:2 * share, LANES:]
        grad_re, grad_im = freq[2 * share:, :LANES], freq[2 * share:, LANES:]
        factor = scale * 0.5 if k1 in (0, blocks) else scale
        grad_re, grad_im = grad_re * factor, grad_im * factor
        filt_scaled_re, filt_scaled_im = filt_re * factor, filt_im * factor
        conv = jnp.concatenate([
            filt_scaled_re * mixed_re - filt_scaled_im * mixed_im,
            filt_scaled_re * mixed_im + filt_scaled_im * mixed_re], axis=1)
        back = jnp.concatenate([
            filt_re * grad_re + filt_im * grad_im, filt_re * grad_im - filt_im * grad_re], axis=1)
        lag = jnp.concatenate([
            mixed_re * grad_re + mixed_im * grad_im, mixed_re * grad_im - mixed_im * grad_re], axis=1)
        products = jnp.concatenate([conv, back, lag], axis=0)
        inverted[k1] = dot_parts(products, high[k1], low[k1], 1)

    def backward(tile, carry):
        at = pl.ds(pl.multiple_of(tile * 8, 8), 8)
        spec = {k1: (inverted[k1, at, :LANES], inverted[k1, at, LANES:]) for k1 in range(blocks + 1)}
        for p, value in enumerate(real_inverse(spec, rows_all, True)):
            result[p, at, :] = value
        return carry

    lax.fori_loop(0, rows // 8, backward, 0)


def unpack_kernel(seq_len, returned, gate_in, values_in, skip_gain, grad_out, gate_out,
                  grad_gate_out, grad_gate_in, grad_values, grad_filter):
    share = returned.shape[1] // 3
    for lane in range(0, gate_in.shape[1], LANES):
        at = slice(lane, lane + LANES)
        values, gate = values_in[:, at].astype(jnp.float32), gate_in[:, at].astype(jnp.float32)
        cotangent = grad_out[:, at].astype(jnp.float32)
        skip = skip_gain[:, at]

        def turned(s):
            return jnp.concatenate(
                [returned[lane // share + b, s * share:(s + 1) * share, :] for b in range(LANES // share)],
                axis=0).T

        mixer_state = turned(0) + skip * (gate * values)
        grad_gate_out[:, at] = (cotangent * mixer_state).astype(jnp.bfloat16)
        grad_mix = turned(1) + skip * (cotangent * gate_out[:, at].astype(jnp.float32))
        grad_gate_in[:, at] = (grad_mix * values).astype(jnp.bfloat16)
        grad_values[:, at] = (grad_mix * gate).astype(jnp.bfloat16)
        grad_filter[:, at] = turned(2) * (1.0 / math.sqrt(seq_len))


def pack(width, devices, gate_in, values_in, long_filter, grad_out, gate_out):
    tokens, channels = gate_in.shape
    share = channels // devices
    rows = 3 * share
    plain = pl.BlockSpec((tokens, width), lambda i: (0, i))
    return pl.pallas_call(
        lambda *refs: pack_kernel(share, *refs),
        grid=(channels // width,),
        in_specs=[plain] * 5,
        out_specs=pl.BlockSpec((width // share, rows, tokens), lambda i: (i, 0, 0)),
        out_shape=jax.ShapeDtypeStruct((devices, rows, tokens), jnp.float32),
        name="pack",
    )(gate_in, values_in, long_filter, grad_out, gate_out)


def convolve(received, high, low):
    blocks, rows, _ = received.shape
    return pl.pallas_call(
        convolve_kernel,
        out_shape=jax.ShapeDtypeStruct(received.shape, jnp.float32),
        in_specs=[pl.BlockSpec(memory_space=pltpu.VMEM)] * 3,
        out_specs=pl.BlockSpec(memory_space=pltpu.VMEM),
        scratch_shapes=[pltpu.VMEM((blocks + 1, rows, 2 * LANES), jnp.float32)] * 2,
        compiler_params=pltpu.CompilerParams(vmem_limit_bytes=40 * 1024 * 1024),
        name="convolve",
    )(received, high, low)


def unpack(width, seq_len, returned, gate_in, values_in, skip_gain, grad_out, gate_out):
    devices, rows, tokens = returned.shape
    channels = gate_in.shape[1]
    share = channels // devices
    plain = pl.BlockSpec((tokens, width), lambda i: (0, i))
    wide = [jax.ShapeDtypeStruct((tokens, channels), jnp.bfloat16)] * 3
    return tuple(pl.pallas_call(
        lambda *refs: unpack_kernel(seq_len, *refs),
        grid=(channels // width,),
        in_specs=[pl.BlockSpec((width // share, rows, tokens), lambda i: (i, 0, 0)), plain, plain,
                  pl.BlockSpec((1, width), lambda i: (0, i)), plain, plain],
        out_specs=[plain] * 4,
        out_shape=wide + [jax.ShapeDtypeStruct((tokens, channels), jnp.float32)],
        name="unpack",
    )(returned, gate_in, values_in, skip_gain[None, :], grad_out, gate_out))


PACK_WIDTH = 512
UNPACK_WIDTH = 512


def local(gate_out, gate_in, values_in, long_filter, skip_gain, grad_out):
    tokens = gate_out.shape[0]
    blocks = lax.axis_size("context")
    high, low = (jnp.asarray(t) for t in table(blocks))
    packed = pack(PACK_WIDTH, blocks, gate_in, values_in, long_filter, grad_out, gate_out)
    received = lax.all_to_all(packed, "context", split_axis=0, concat_axis=0, tiled=True)
    result = convolve(received, high, low)
    returned = lax.all_to_all(result, "context", split_axis=0, concat_axis=0, tiled=True)
    return unpack(UNPACK_WIDTH, tokens * blocks, returned, gate_in, values_in, skip_gain, grad_out, gate_out)


def solution(mesh):
    sequence = P(("dp", "context"), "tensor")
    return jax.shard_map(
        local,
        mesh=mesh,
        in_specs=(sequence, sequence, sequence, P("context", "tensor"), P("tensor"), sequence),
        out_specs=(sequence,) * 4,
        check_vma=False,
    )
```

```python
import math

import jax
import jax.numpy as jnp
import numpy as np
from jax import lax
from jax.experimental import pallas as pl
from jax.experimental.pallas import tpu as pltpu
from jax.sharding import PartitionSpec as P

LANES = 128
AXES = ("line", "dp", "column")


def complex_add(a, b):
    return (a[0] + b[0], a[1] + b[1])


def complex_sub(a, b):
    return (a[0] - b[0], a[1] - b[1])


def rotate(a, angle_num, angle_den):
    num = angle_num % angle_den
    re, im = a
    if num == 0:
        return a
    if 4 * num == angle_den:
        return (-im, re)
    if 2 * num == angle_den:
        return (-re, -im)
    if 4 * num == 3 * angle_den:
        return (im, -re)
    if (8 * num) % angle_den == 0:
        half = math.sqrt(0.5)
        octant = (8 * num) // angle_den
        if octant == 1:
            return ((re - im) * half, (re + im) * half)
        if octant == 3:
            return ((re + im) * -half, (re - im) * half)
        if octant == 5:
            return ((im - re) * half, (re + im) * -half)
        return ((re + im) * half, (im - re) * half)
    c = math.cos(2.0 * math.pi * num / angle_den)
    s = math.sin(2.0 * math.pi * num / angle_den)
    return (re * c - im * s, re * s + im * c)


def complex_fft(values, sign):
    n = len(values)
    if n == 1:
        return values
    half = n // 2
    sums = [complex_add(values[p], values[p + half]) for p in range(half)]
    diffs = [complex_sub(values[p], values[p + half]) for p in range(half)]
    diffs = [rotate(d, sign * p, n) for p, d in enumerate(diffs)]
    even = complex_fft(sums, sign)
    odd = complex_fft(diffs, sign)
    return [v for pair in zip(even, odd) for v in pair]


def odd_forward(diffs, n, out):
    quarter = n // 4
    if n == 2:
        out[1] = (diffs[0], None)
        return
    twisted = [rotate((diffs[p], -diffs[p + quarter]), -p, n) for p in range(quarter)]
    for r, value in enumerate(complex_fft(twisted, -1)):
        k = 4 * r + 1
        if 2 * k < n:
            out[k] = value
        else:
            out[n - k] = (value[0], -value[1])


def real_forward(values, n):
    out = {}
    half = n // 2
    if len(values) == half:
        sums, diffs = values, values
    else:
        sums = [values[p] + values[p + half] for p in range(half)]
        diffs = [values[p] - values[p + half] for p in range(half)]
    if half == 1:
        out[0] = (sums[0], None)
    else:
        for k, value in real_forward(sums, half).items():
            out[2 * k] = value
    odd_forward(diffs, n, out)
    return out


def real_inverse(spec, n, first_half):
    half, quarter = n // 2, n // 4
    if n == 2:
        return [spec[0][0] + spec[1][0], spec[0][0] - spec[1][0]]
    evens = real_inverse({k // 2: v for k, v in spec.items() if k % 2 == 0}, half, False)
    odds = []
    for r in range(quarter):
        k = 4 * r + 1
        odds.append(spec[k] if 2 * k < n else (spec[n - k][0], -spec[n - k][1]))
    turned = [rotate(v, p, n) for p, v in enumerate(complex_fft(odds, 1))]
    odd_part = [v[0] for v in turned] + [-v[1] for v in turned]
    front = [evens[p] + odd_part[p] for p in range(half)]
    if first_half:
        return front
    return front + [evens[p] - odd_part[p] for p in range(half)]


def table(blocks):
    rows_all = 2 * blocks
    length = rows_all * LANES
    lane = np.arange(LANES)
    out = []
    for k1 in range(blocks + 1):
        angles = 2.0 * np.pi * (lane[:, None] * (k1 + rows_all * lane[None, :]) % length) / length
        cosine, sine = np.cos(angles), np.sin(angles)
        out.append(np.block([[cosine, -sine], [sine, cosine]]))
    whole = np.stack(out).astype(np.float32)
    high = whole.astype(jnp.bfloat16)
    low = (whole - high.astype(np.float32)).astype(jnp.bfloat16)
    return high, low


def split(value):
    high = value.astype(jnp.bfloat16)
    return high, (value - high.astype(jnp.float32)).astype(jnp.bfloat16)


def dot_parts(left, right_high, right_low, right_dim):
    dims = (((1,), (right_dim,)), ((), ()))
    high, low = split(left)
    total = lax.dot_general(low, right_high, dims, preferred_element_type=jnp.float32)
    total += lax.dot_general(high, right_low, dims, preferred_element_type=jnp.float32)
    return total + lax.dot_general(high, right_high, dims, preferred_element_type=jnp.float32)


def rows_of(signal, share, parts):
    return share // parts if signal == FILTER else share


def pack_kernel(share, parts, plan, gate_in, values_in, long_filter, grad_out, gate_out, *packed):
    mixed = gate_in[...].astype(jnp.float32) * values_in[...].astype(jnp.float32)
    grad = grad_out[...].astype(jnp.float32) * gate_out[...].astype(jnp.float32)
    signals = {MIXED: mixed, FILTER: long_filter[...].astype(jnp.float32), GRAD: grad}
    part = lax.axis_index("dp")
    for out, members in zip(packed, plan):
        given = 0
        for signal in members:
            count = rows_of(signal, share, parts)
            for lane in range(0, mixed.shape[1], LANES):
                turned = signals[signal][:, lane:lane + LANES].T
                for b in range(LANES // share):
                    kept = turned[b * share:b * share + count]
                    for other in range(1, share // count):
                        start = b * share + other * count
                        kept = jnp.where(part == other, turned[start:start + count], kept)
                    out[lane // share + b, given:given + count, :] = kept
            given += count


def convolve_kernel(shape, plan, *refs):
    received, (high, low, result, spectrum, inverted) = refs[:len(plan)], refs[len(plan):]
    lines, parts, columns = shape
    blocks = lines * columns
    share = result.shape[1] // 3
    rows_all = 2 * blocks
    scale = 2.0 / (rows_all * LANES)
    grad_row, filt_row = parts * share, 2 * parts * share
    first_row = {MIXED: 0, GRAD: grad_row, FILTER: filt_row}

    def source(line, part, column):
        return (line * parts + part) * columns + column

    for operand, members in zip(received, plan):
        taken_row = 0
        for signal in members:
            count = rows_of(signal, share, parts)
            for part in range(parts):
                given_row = first_row[signal] + part * count

                def forward(tile, carry):
                    taken = pl.ds(pl.multiple_of(taken_row + tile * 8, 8), 8)
                    given = pl.ds(pl.multiple_of(given_row + tile * 8, 8), 8)
                    out = real_forward(
                        [operand[source(x, part, z), taken, :] for x in range(lines) for z in range(columns)],
                        rows_all)
                    for k1 in range(blocks + 1):
                        re, im = out[k1]
                        spectrum[k1, given, :LANES] = re
                        spectrum[k1, given, LANES:] = jnp.zeros_like(re) if im is None else im
                    return carry

                lax.fori_loop(0, count // 8, forward, 0)
            taken_row += count

    for k1 in range(blocks + 1):
        freq = dot_parts(spectrum[k1], high[k1], low[k1], 0)
        factor = scale * 0.5 if k1 in (0, blocks) else scale
        filt_re, filt_im = freq[filt_row:, :LANES], freq[filt_row:, LANES:]
        filt_re, filt_im = filt_re * factor, filt_im * factor
        products = []
        for part in range(parts):
            mixed = slice(part * share, (part + 1) * share)
            grad = slice(grad_row + part * share, grad_row + (part + 1) * share)
            mixed_re, mixed_im = freq[mixed, :LANES], freq[mixed, LANES:]
            grad_re, grad_im = freq[grad, :LANES], freq[grad, LANES:]
            products.append(jnp.concatenate([
                filt_re * mixed_re - filt_im * mixed_im, filt_re * mixed_im + filt_im * mixed_re], axis=1))
            products.append(jnp.concatenate([
                filt_re * grad_re + filt_im * grad_im, filt_re * grad_im - filt_im * grad_re], axis=1))
            mixed_re, mixed_im = mixed_re * factor, mixed_im * factor
            products.append(jnp.concatenate([
                mixed_re * grad_re + mixed_im * grad_im, mixed_re * grad_im - mixed_im * grad_re], axis=1))
        inverted[k1] = dot_parts(jnp.concatenate(products, axis=0), high[k1], low[k1], 1)

    for part in range(parts):
        def backward(tile, carry):
            start = pl.multiple_of(tile * 8, 8)
            at = pl.ds(pl.multiple_of(part * 3 * share + start, 8), 8)
            spec = {k1: (inverted[k1, at, :LANES], inverted[k1, at, LANES:]) for k1 in range(blocks + 1)}
            values = real_inverse(spec, rows_all, True)
            for x in range(lines):
                for z in range(columns):
                    result[source(x, part, z), pl.ds(start, 8), :] = values[x * columns + z]
            return carry

        lax.fori_loop(0, 3 * share // 8, backward, 0)


def unpack_kernel(seq_len, returned, gate_in, values_in, skip_gain, grad_out, gate_out,
                  grad_gate_out, grad_gate_in, grad_values, grad_filter):
    share = returned.shape[1] // 3
    for lane in range(0, gate_in.shape[1], LANES):
        at = slice(lane, lane + LANES)
        values, gate = values_in[:, at].astype(jnp.float32), gate_in[:, at].astype(jnp.float32)
        cotangent = grad_out[:, at].astype(jnp.float32)
        skip = skip_gain[:, at]

        def turned(s):
            return jnp.concatenate(
                [returned[lane // share + b, s * share:(s + 1) * share, :] for b in range(LANES // share)],
                axis=0).T

        mixer_state = turned(0) + skip * (gate * values)
        grad_gate_out[:, at] = (cotangent * mixer_state).astype(jnp.bfloat16)
        grad_mix = turned(1) + skip * (cotangent * gate_out[:, at].astype(jnp.float32))
        grad_gate_in[:, at] = (grad_mix * values).astype(jnp.bfloat16)
        grad_values[:, at] = (grad_mix * gate).astype(jnp.bfloat16)
        grad_filter[:, at] = turned(2) * (1.0 / math.sqrt(seq_len))


def pack(width, devices, parts, plan, gate_in, values_in, long_filter, grad_out, gate_out):
    tokens, channels = gate_in.shape
    share = channels // devices
    rows = [sum(rows_of(signal, share, parts) for signal in members) for members in plan]
    plain = pl.BlockSpec((tokens, width), lambda i: (0, i))
    return pl.pallas_call(
        lambda *refs: pack_kernel(share, parts, plan, *refs),
        grid=(channels // width,),
        in_specs=[plain] * 5,
        out_specs=[pl.BlockSpec((width // share, r, tokens), lambda i: (i, 0, 0)) for r in rows],
        out_shape=[jax.ShapeDtypeStruct((devices, r, tokens), jnp.float32) for r in rows],
        name="pack",
    )(gate_in, values_in, long_filter, grad_out, gate_out)


def convolve(shape, share, plan, received, high, low):
    devices, _, tokens = received[0].shape
    blocks = shape[0] * shape[2]
    forward_rows = (2 * shape[1] + 1) * share
    inverse_rows = 3 * shape[1] * share
    return pl.pallas_call(
        lambda *refs: convolve_kernel(shape, plan, *refs),
        out_shape=jax.ShapeDtypeStruct((devices, 3 * share, tokens), jnp.float32),
        in_specs=[pl.BlockSpec(memory_space=pltpu.VMEM)] * (len(plan) + 2),
        out_specs=pl.BlockSpec(memory_space=pltpu.VMEM),
        scratch_shapes=[pltpu.VMEM((blocks + 1, forward_rows, 2 * LANES), jnp.float32),
                        pltpu.VMEM((blocks + 1, inverse_rows, 2 * LANES), jnp.float32)],
        compiler_params=pltpu.CompilerParams(vmem_limit_bytes=40 * 1024 * 1024),
        name="convolve",
    )(*received, high, low)


def unpack(width, seq_len, returned, gate_in, values_in, skip_gain, grad_out, gate_out):
    devices, rows, tokens = returned.shape
    channels = gate_in.shape[1]
    share = channels // devices
    plain = pl.BlockSpec((tokens, width), lambda i: (0, i))
    wide = [jax.ShapeDtypeStruct((tokens, channels), jnp.bfloat16)] * 3
    return tuple(pl.pallas_call(
        lambda *refs: unpack_kernel(seq_len, *refs),
        grid=(channels // width,),
        in_specs=[pl.BlockSpec((width // share, rows, tokens), lambda i: (i, 0, 0)), plain, plain,
                  pl.BlockSpec((1, width), lambda i: (0, i)), plain, plain],
        out_specs=[plain] * 4,
        out_shape=wide + [jax.ShapeDtypeStruct((tokens, channels), jnp.float32)],
        name="unpack",
    )(returned, gate_in, values_in, skip_gain[None, :], grad_out, gate_out))


PACK_WIDTH = 512
UNPACK_WIDTH = 512
MIXED, FILTER, GRAD = 0, 1, 2
WHOLE = ((MIXED, FILTER, GRAD),)
FILTER_FIRST = ((FILTER,), (MIXED, GRAD))


def local(gate_out, gate_in, values_in, long_filter, skip_gain, grad_out):
    tokens, channels = gate_out.shape
    shape = tuple(lax.axis_size(axis) for axis in AXES)
    devices = math.prod(shape)
    blocks = shape[0] * shape[2]
    high, low = (jnp.asarray(t) for t in table(blocks))

    def exchange(operand):
        return lax.all_to_all(operand, AXES, split_axis=0, concat_axis=0, tiled=True)

    def there_and_back(plan):
        def run(*operands):
            packed = pack(PACK_WIDTH, devices, shape[1], plan, *operands)
            received = [exchange(packed[0])]
            for part in packed[1:]:
                part, _ = lax.optimization_barrier((part, received[-1][0, 0, 0]))
                received.append(exchange(part))
            return exchange(convolve(shape, channels // devices, plan, received, high, low))
        return run

    returned = lax.cond(
        lax.axis_index("tensor") % 2 == 0, there_and_back(WHOLE), there_and_back(FILTER_FIRST),
        gate_in, values_in, long_filter, grad_out, gate_out)
    return unpack(UNPACK_WIDTH, tokens * blocks, returned, gate_in, values_in, skip_gain, grad_out, gate_out)


def solution(mesh):
    parts, tensor, context = mesh.devices.shape
    lines = 2
    mesh = jax.sharding.Mesh(
        mesh.devices.reshape(parts, tensor, lines, context // lines), ("dp", "tensor", "line", "column"))
    sequence = P(("dp", "line", "column"), "tensor")
    return jax.shard_map(
        local,
        mesh=mesh,
        in_specs=(sequence, sequence, sequence, P(("line", "column"), "tensor"), P("tensor"), sequence),
        out_specs=(sequence,) * 4,
        check_vma=False,
    )
```

```python
import math

import jax
import jax.numpy as jnp
import numpy as np
from jax import lax
from jax.experimental import pallas as pl
from jax.experimental.pallas import tpu as pltpu
from jax.sharding import PartitionSpec as P

LANES = 128
AXES = ("line", "dp", "column")


def complex_add(a, b):
    return (a[0] + b[0], a[1] + b[1])


def complex_sub(a, b):
    return (a[0] - b[0], a[1] - b[1])


def rotate(a, angle_num, angle_den):
    num = angle_num % angle_den
    re, im = a
    if num == 0:
        return a
    if 4 * num == angle_den:
        return (-im, re)
    if 2 * num == angle_den:
        return (-re, -im)
    if 4 * num == 3 * angle_den:
        return (im, -re)
    if (8 * num) % angle_den == 0:
        half = math.sqrt(0.5)
        octant = (8 * num) // angle_den
        if octant == 1:
            return ((re - im) * half, (re + im) * half)
        if octant == 3:
            return ((re + im) * -half, (re - im) * half)
        if octant == 5:
            return ((im - re) * half, (re + im) * -half)
        return ((re + im) * half, (im - re) * half)
    c = math.cos(2.0 * math.pi * num / angle_den)
    s = math.sin(2.0 * math.pi * num / angle_den)
    return (re * c - im * s, re * s + im * c)


def complex_fft(values, sign):
    n = len(values)
    if n == 1:
        return values
    half = n // 2
    sums = [complex_add(values[p], values[p + half]) for p in range(half)]
    diffs = [complex_sub(values[p], values[p + half]) for p in range(half)]
    diffs = [rotate(d, sign * p, n) for p, d in enumerate(diffs)]
    even = complex_fft(sums, sign)
    odd = complex_fft(diffs, sign)
    return [v for pair in zip(even, odd) for v in pair]


def odd_forward(diffs, n, out):
    quarter = n // 4
    if n == 2:
        out[1] = (diffs[0], None)
        return
    twisted = [rotate((diffs[p], -diffs[p + quarter]), -p, n) for p in range(quarter)]
    for r, value in enumerate(complex_fft(twisted, -1)):
        k = 4 * r + 1
        if 2 * k < n:
            out[k] = value
        else:
            out[n - k] = (value[0], -value[1])


def real_forward(values, n):
    out = {}
    half = n // 2
    if len(values) == half:
        sums, diffs = values, values
    else:
        sums = [values[p] + values[p + half] for p in range(half)]
        diffs = [values[p] - values[p + half] for p in range(half)]
    if half == 1:
        out[0] = (sums[0], None)
    else:
        for k, value in real_forward(sums, half).items():
            out[2 * k] = value
    odd_forward(diffs, n, out)
    return out


def real_inverse(spec, n, first_half):
    half, quarter = n // 2, n // 4
    if n == 2:
        return [spec[0][0] + spec[1][0], spec[0][0] - spec[1][0]]
    evens = real_inverse({k // 2: v for k, v in spec.items() if k % 2 == 0}, half, False)
    odds = []
    for r in range(quarter):
        k = 4 * r + 1
        odds.append(spec[k] if 2 * k < n else (spec[n - k][0], -spec[n - k][1]))
    turned = [rotate(v, p, n) for p, v in enumerate(complex_fft(odds, 1))]
    odd_part = [v[0] for v in turned] + [-v[1] for v in turned]
    front = [evens[p] + odd_part[p] for p in range(half)]
    if first_half:
        return front
    return front + [evens[p] - odd_part[p] for p in range(half)]


def table(blocks):
    rows_all = 2 * blocks
    length = rows_all * LANES
    lane = np.arange(LANES)
    out = []
    for k1 in range(blocks + 1):
        angles = 2.0 * np.pi * (lane[:, None] * (k1 + rows_all * lane[None, :]) % length) / length
        cosine, sine = np.cos(angles), np.sin(angles)
        out.append(np.block([[cosine, -sine], [sine, cosine]]))
    whole = np.stack(out).astype(np.float32)
    high = whole.astype(jnp.bfloat16)
    low = (whole - high.astype(np.float32)).astype(jnp.bfloat16)
    return high, low


def split(value):
    high = value.astype(jnp.bfloat16)
    return high, (value - high.astype(jnp.float32)).astype(jnp.bfloat16)


def dot_parts(left, right_high, right_low, right_dim):
    dims = (((1,), (right_dim,)), ((), ()))
    high, low = split(left)
    total = lax.dot_general(low, right_high, dims, preferred_element_type=jnp.float32)
    total += lax.dot_general(high, right_low, dims, preferred_element_type=jnp.float32)
    return total + lax.dot_general(high, right_high, dims, preferred_element_type=jnp.float32)


def rows_of(signal, share, parts):
    return share // parts if signal == FILTER else share


def pack_kernel(share, parts, members, *refs):
    packed = refs[-1]
    part = lax.axis_index("dp")
    used = given = 0
    for signal in members:
        factors = refs[used:used + FACTORS[signal]]
        used += FACTORS[signal]
        count = rows_of(signal, share, parts)
        for lane in range(0, packed.shape[0] * share, LANES):
            value = factors[0][:, lane:lane + LANES].astype(jnp.float32)
            for factor in factors[1:]:
                value *= factor[:, lane:lane + LANES].astype(jnp.float32)
            turned = value.T
            for b in range(LANES // share):
                kept = turned[b * share:b * share + count]
                for other in range(1, share // count):
                    start = b * share + other * count
                    kept = jnp.where(part == other, turned[start:start + count], kept)
                packed[lane // share + b, given:given + count, :] = kept
        given += count


def convolve_kernel(shape, plan, *refs):
    received, (high, low, result, spectrum, inverted) = refs[:len(plan)], refs[len(plan):]
    lines, parts, columns = shape
    blocks = lines * columns
    share = result.shape[1] // 3
    rows_all = 2 * blocks
    scale = 2.0 / (rows_all * LANES)
    grad_row, filt_row = parts * share, 2 * parts * share
    first_row = {MIXED: 0, GRAD: grad_row, FILTER: filt_row}

    def source(line, part, column):
        return (line * parts + part) * columns + column

    for operand, members in zip(received, plan):
        taken_row = 0
        for signal in members:
            count = rows_of(signal, share, parts)
            for part in range(parts):
                given_row = first_row[signal] + part * count

                def forward(tile, carry):
                    taken = pl.ds(pl.multiple_of(taken_row + tile * 8, 8), 8)
                    given = pl.ds(pl.multiple_of(given_row + tile * 8, 8), 8)
                    out = real_forward(
                        [operand[source(x, part, z), taken, :] for x in range(lines) for z in range(columns)],
                        rows_all)
                    for k1 in range(blocks + 1):
                        re, im = out[k1]
                        spectrum[k1, given, :LANES] = re
                        spectrum[k1, given, LANES:] = jnp.zeros_like(re) if im is None else im
                    return carry

                lax.fori_loop(0, count // 8, forward, 0)
            taken_row += count

    for k1 in range(blocks + 1):
        freq = dot_parts(spectrum[k1], high[k1], low[k1], 0)
        factor = scale * 0.5 if k1 in (0, blocks) else scale
        filt_re, filt_im = freq[filt_row:, :LANES], freq[filt_row:, LANES:]
        filt_re, filt_im = filt_re * factor, filt_im * factor
        products = []
        for part in range(parts):
            mixed = slice(part * share, (part + 1) * share)
            grad = slice(grad_row + part * share, grad_row + (part + 1) * share)
            mixed_re, mixed_im = freq[mixed, :LANES], freq[mixed, LANES:]
            grad_re, grad_im = freq[grad, :LANES], freq[grad, LANES:]
            products.append(jnp.concatenate([
                filt_re * mixed_re - filt_im * mixed_im, filt_re * mixed_im + filt_im * mixed_re], axis=1))
            products.append(jnp.concatenate([
                filt_re * grad_re + filt_im * grad_im, filt_re * grad_im - filt_im * grad_re], axis=1))
            mixed_re, mixed_im = mixed_re * factor, mixed_im * factor
            products.append(jnp.concatenate([
                mixed_re * grad_re + mixed_im * grad_im, mixed_re * grad_im - mixed_im * grad_re], axis=1))
        inverted[k1] = dot_parts(jnp.concatenate(products, axis=0), high[k1], low[k1], 1)

    for part in range(parts):
        def backward(tile, carry):
            start = pl.multiple_of(tile * 8, 8)
            at = pl.ds(pl.multiple_of(part * 3 * share + start, 8), 8)
            spec = {k1: (inverted[k1, at, :LANES], inverted[k1, at, LANES:]) for k1 in range(blocks + 1)}
            values = real_inverse(spec, rows_all, True)
            for x in range(lines):
                for z in range(columns):
                    result[source(x, part, z), pl.ds(start, 8), :] = values[x * columns + z]
            return carry

        lax.fori_loop(0, 3 * share // 8, backward, 0)


def unpack_kernel(seq_len, returned, gate_in, values_in, skip_gain, grad_out, gate_out,
                  grad_gate_out, grad_gate_in, grad_values, grad_filter):
    share = returned.shape[1] // 3
    for lane in range(0, gate_in.shape[1], LANES):
        at = slice(lane, lane + LANES)
        values, gate = values_in[:, at].astype(jnp.float32), gate_in[:, at].astype(jnp.float32)
        cotangent = grad_out[:, at].astype(jnp.float32)
        skip = skip_gain[:, at]

        def turned(s):
            return jnp.concatenate(
                [returned[lane // share + b, s * share:(s + 1) * share, :] for b in range(LANES // share)],
                axis=0).T

        mixer_state = turned(0) + skip * (gate * values)
        grad_gate_out[:, at] = (cotangent * mixer_state).astype(jnp.bfloat16)
        grad_mix = turned(1) + skip * (cotangent * gate_out[:, at].astype(jnp.float32))
        grad_gate_in[:, at] = (grad_mix * values).astype(jnp.bfloat16)
        grad_values[:, at] = (grad_mix * gate).astype(jnp.bfloat16)
        grad_filter[:, at] = turned(2) * (1.0 / math.sqrt(seq_len))


def pack(width, devices, parts, members, signals):
    operands = [factor for signal in members for factor in signals[signal]]
    tokens, channels = operands[0].shape
    share = channels // devices
    rows = sum(rows_of(signal, share, parts) for signal in members)
    return pl.pallas_call(
        lambda *refs: pack_kernel(share, parts, members, *refs),
        grid=(channels // width,),
        in_specs=[pl.BlockSpec((tokens, width), lambda i: (0, i))] * len(operands),
        out_specs=pl.BlockSpec((width // share, rows, tokens), lambda i: (i, 0, 0)),
        out_shape=jax.ShapeDtypeStruct((devices, rows, tokens), jnp.float32),
        compiler_params=pltpu.CompilerParams(vmem_limit_bytes=16 * 1024 * 1024),
        name="pack",
    )(*operands)


def convolve(shape, share, plan, received, high, low):
    devices, _, tokens = received[0].shape
    blocks = shape[0] * shape[2]
    forward_rows = (2 * shape[1] + 1) * share
    inverse_rows = 3 * shape[1] * share
    return pl.pallas_call(
        lambda *refs: convolve_kernel(shape, plan, *refs),
        out_shape=jax.ShapeDtypeStruct((devices, 3 * share, tokens), jnp.float32),
        in_specs=[pl.BlockSpec(memory_space=pltpu.VMEM)] * (len(plan) + 2),
        out_specs=pl.BlockSpec(memory_space=pltpu.VMEM),
        scratch_shapes=[pltpu.VMEM((blocks + 1, forward_rows, 2 * LANES), jnp.float32),
                        pltpu.VMEM((blocks + 1, inverse_rows, 2 * LANES), jnp.float32)],
        compiler_params=pltpu.CompilerParams(vmem_limit_bytes=24 * 1024 * 1024),
        name="convolve",
    )(*received, high, low)


def unpack(width, seq_len, returned, gate_in, values_in, skip_gain, grad_out, gate_out):
    devices, rows, tokens = returned.shape
    channels = gate_in.shape[1]
    share = channels // devices
    plain = pl.BlockSpec((tokens, width), lambda i: (0, i))
    wide = [jax.ShapeDtypeStruct((tokens, channels), jnp.bfloat16)] * 3
    return tuple(pl.pallas_call(
        lambda *refs: unpack_kernel(seq_len, *refs),
        grid=(channels // width,),
        in_specs=[pl.BlockSpec((width // share, rows, tokens), lambda i: (i, 0, 0)), plain, plain,
                  pl.BlockSpec((1, width), lambda i: (0, i)), plain, plain],
        out_specs=[plain] * 4,
        out_shape=wide + [jax.ShapeDtypeStruct((tokens, channels), jnp.float32)],
        compiler_params=pltpu.CompilerParams(vmem_limit_bytes=16 * 1024 * 1024),
        name="unpack",
    )(returned, gate_in, values_in, skip_gain[None, :], grad_out, gate_out))


PACK_WIDTH = 512
UNPACK_WIDTH = 512
MIXED, FILTER, GRAD = 0, 1, 2
FACTORS = (2, 1, 2)
WHOLE = ((MIXED, FILTER, GRAD),)
FILTER_FIRST = ((FILTER,), (MIXED, GRAD))


def local(gate_out, gate_in, values_in, long_filter, skip_gain, grad_out):
    tokens, channels = gate_out.shape
    shape = tuple(lax.axis_size(axis) for axis in AXES)
    devices = math.prod(shape)
    blocks = shape[0] * shape[2]
    high, low = (jnp.asarray(t) for t in table(blocks))

    def exchange(operand):
        return lax.all_to_all(operand, AXES, split_axis=0, concat_axis=0, tiled=True)

    def there_and_back(plan):
        def run(gate_out, gate_in, values_in, long_filter, skip_gain, grad_out):
            signals = {MIXED: (gate_in, values_in), FILTER: (long_filter,), GRAD: (grad_out, gate_out)}
            received = []
            for members in plan:
                part = pack(PACK_WIDTH, devices, shape[1], members, signals)
                if received:
                    part, _ = lax.optimization_barrier((part, received[-1][0, 0, 0]))
                received.append(exchange(part))
            returned = exchange(convolve(shape, channels // devices, plan, received, high, low))
            return unpack(UNPACK_WIDTH, tokens * blocks, returned, gate_in, values_in, skip_gain, grad_out, gate_out)
        return run

    return lax.cond(
        lax.axis_index("tensor") % 2 == 0, there_and_back(WHOLE), there_and_back(FILTER_FIRST),
        gate_out, gate_in, values_in, long_filter, skip_gain, grad_out)


def solution(mesh):
    parts, tensor, context = mesh.devices.shape
    lines = 2
    mesh = jax.sharding.Mesh(
        mesh.devices.reshape(parts, tensor, lines, context // lines), ("dp", "tensor", "line", "column"))
    sequence = P(("dp", "line", "column"), "tensor")
    return jax.shard_map(
        local,
        mesh=mesh,
        in_specs=(sequence, sequence, sequence, P(("line", "column"), "tensor"), P("tensor"), sequence),
        out_specs=(sequence,) * 4,
        check_vma=False,
    )
```

```python
import math

import jax
import jax.numpy as jnp
import numpy as np
from jax import lax
from jax.experimental import pallas as pl
from jax.experimental.pallas import tpu as pltpu
from jax.sharding import PartitionSpec as P

LANES = 128
AXES = ("line", "dp", "column")


def complex_add(a, b):
    return (a[0] + b[0], a[1] + b[1])


def complex_sub(a, b):
    return (a[0] - b[0], a[1] - b[1])


def rotate(a, angle_num, angle_den):
    num = angle_num % angle_den
    re, im = a
    if num == 0:
        return a
    if 4 * num == angle_den:
        return (-im, re)
    if 2 * num == angle_den:
        return (-re, -im)
    if 4 * num == 3 * angle_den:
        return (im, -re)
    if (8 * num) % angle_den == 0:
        half = math.sqrt(0.5)
        octant = (8 * num) // angle_den
        if octant == 1:
            return ((re - im) * half, (re + im) * half)
        if octant == 3:
            return ((re + im) * -half, (re - im) * half)
        if octant == 5:
            return ((im - re) * half, (re + im) * -half)
        return ((re + im) * half, (im - re) * half)
    c = math.cos(2.0 * math.pi * num / angle_den)
    s = math.sin(2.0 * math.pi * num / angle_den)
    return (re * c - im * s, re * s + im * c)


def complex_fft(values, sign):
    n = len(values)
    if n == 1:
        return values
    half = n // 2
    sums = [complex_add(values[p], values[p + half]) for p in range(half)]
    diffs = [complex_sub(values[p], values[p + half]) for p in range(half)]
    diffs = [rotate(d, sign * p, n) for p, d in enumerate(diffs)]
    even = complex_fft(sums, sign)
    odd = complex_fft(diffs, sign)
    return [v for pair in zip(even, odd) for v in pair]


def odd_forward(diffs, n, out):
    quarter = n // 4
    if n == 2:
        out[1] = (diffs[0], None)
        return
    twisted = [rotate((diffs[p], -diffs[p + quarter]), -p, n) for p in range(quarter)]
    for r, value in enumerate(complex_fft(twisted, -1)):
        k = 4 * r + 1
        if 2 * k < n:
            out[k] = value
        else:
            out[n - k] = (value[0], -value[1])


def real_forward(values, n):
    out = {}
    half = n // 2
    if len(values) == half:
        sums, diffs = values, values
    else:
        sums = [values[p] + values[p + half] for p in range(half)]
        diffs = [values[p] - values[p + half] for p in range(half)]
    if half == 1:
        out[0] = (sums[0], None)
    else:
        for k, value in real_forward(sums, half).items():
            out[2 * k] = value
    odd_forward(diffs, n, out)
    return out


def real_inverse(spec, n, first_half):
    half, quarter = n // 2, n // 4
    if n == 2:
        return [spec[0][0] + spec[1][0], spec[0][0] - spec[1][0]]
    evens = real_inverse({k // 2: v for k, v in spec.items() if k % 2 == 0}, half, False)
    odds = []
    for r in range(quarter):
        k = 4 * r + 1
        odds.append(spec[k] if 2 * k < n else (spec[n - k][0], -spec[n - k][1]))
    turned = [rotate(v, p, n) for p, v in enumerate(complex_fft(odds, 1))]
    odd_part = [v[0] for v in turned] + [-v[1] for v in turned]
    front = [evens[p] + odd_part[p] for p in range(half)]
    if first_half:
        return front
    return front + [evens[p] - odd_part[p] for p in range(half)]


def tables(blocks):
    rows_all = 2 * blocks
    lane = np.arange(LANES)
    angles = 2.0 * np.pi * (lane[:, None] * lane[None, :] % LANES) / LANES
    cosine, sine = np.cos(angles), np.sin(angles)
    whole = np.block([[cosine, -sine], [sine, cosine]]).astype(np.float32)
    high = whole.astype(jnp.bfloat16)
    low = (whole - high.astype(np.float32)).astype(jnp.bfloat16)
    turn = 2.0 * np.pi * np.arange(blocks + 1)[:, None] * lane[None, :] / (rows_all * LANES)
    twiddles = np.stack([np.cos(turn), np.sin(turn)], axis=1).astype(np.float32)
    return high, low, np.repeat(twiddles[:, :, None, :], 8, axis=2)


def split(value):
    high = value.astype(jnp.bfloat16)
    return high, (value - high.astype(jnp.float32)).astype(jnp.bfloat16)


def dot_parts(left, right_high, right_low, right_dim):
    dims = (((1,), (right_dim,)), ((), ()))
    high, low = split(left)
    total = lax.dot_general(low, right_high, dims, preferred_element_type=jnp.float32)
    total += lax.dot_general(high, right_low, dims, preferred_element_type=jnp.float32)
    return total + lax.dot_general(high, right_high, dims, preferred_element_type=jnp.float32)


def rows_of(signal, share, parts):
    return share // parts if signal == FILTER else share


def pack_kernel(share, parts, members, *refs):
    packed = refs[-1]
    part = lax.axis_index("dp")
    used = given = 0
    for signal in members:
        factors = refs[used:used + FACTORS[signal]]
        used += FACTORS[signal]
        count = rows_of(signal, share, parts)
        for lane in range(0, packed.shape[0] * share, LANES):
            value = factors[0][:, lane:lane + LANES].astype(jnp.float32)
            for factor in factors[1:]:
                value *= factor[:, lane:lane + LANES].astype(jnp.float32)
            turned = value.T
            for b in range(LANES // share):
                kept = turned[b * share:b * share + count]
                for other in range(1, share // count):
                    start = b * share + other * count
                    kept = jnp.where(part == other, turned[start:start + count], kept)
                packed[lane // share + b, given:given + count, :] = kept
        given += count


def convolve_kernel(shape, plan, *refs):
    received, (high, low, twiddles, result, spectrum, inverted) = refs[:len(plan)], refs[len(plan):]
    lines, parts, columns = shape
    blocks = lines * columns
    share = result.shape[1] // 3
    rows_all = 2 * blocks
    scale = 2.0 / (rows_all * LANES)
    grad_row, filt_row = parts * share, 2 * parts * share
    first_row = {MIXED: 0, GRAD: grad_row, FILTER: filt_row}

    def source(line, part, column):
        return (line * parts + part) * columns + column

    for operand, members in zip(received, plan):
        taken_row = 0
        for signal in members:
            count = rows_of(signal, share, parts)
            for part in range(parts):
                given_row = first_row[signal] + part * count

                def forward(tile, carry):
                    taken = pl.ds(pl.multiple_of(taken_row + tile * 8, 8), 8)
                    given = pl.ds(pl.multiple_of(given_row + tile * 8, 8), 8)
                    out = real_forward(
                        [operand[source(x, part, z), taken, :] for x in range(lines) for z in range(columns)],
                        rows_all)
                    for k1 in range(blocks + 1):
                        re, im = out[k1]
                        cosine, sine = twiddles[k1, 0], twiddles[k1, 1]
                        if im is None:
                            spectrum[k1, given, :LANES] = re * cosine
                            spectrum[k1, given, LANES:] = re * -sine
                        else:
                            spectrum[k1, given, :LANES] = re * cosine + im * sine
                            spectrum[k1, given, LANES:] = im * cosine - re * sine
                    return carry

                lax.fori_loop(0, count // 8, forward, 0)
            taken_row += count

    rows, products_rows = spectrum.shape[1], inverted.shape[1]
    for begin in range(0, blocks + 1, GROUP):
        end = min(begin + GROUP, blocks + 1)
        freqs = dot_parts(spectrum[begin:end].reshape((end - begin) * rows, 2 * LANES), high[...], low[...], 0)
        products = []
        for k1 in range(begin, end):
            freq = freqs[(k1 - begin) * rows:(k1 - begin + 1) * rows]
            factor = scale * 0.5 if k1 in (0, blocks) else scale
            filt_re, filt_im = freq[filt_row:, :LANES], freq[filt_row:, LANES:]
            filt_re, filt_im = filt_re * factor, filt_im * factor
            for part in range(parts):
                mixed = slice(part * share, (part + 1) * share)
                grad = slice(grad_row + part * share, grad_row + (part + 1) * share)
                mixed_re, mixed_im = freq[mixed, :LANES], freq[mixed, LANES:]
                grad_re, grad_im = freq[grad, :LANES], freq[grad, LANES:]
                products.append(jnp.concatenate([
                    filt_re * mixed_re - filt_im * mixed_im, filt_re * mixed_im + filt_im * mixed_re], axis=1))
                products.append(jnp.concatenate([
                    filt_re * grad_re + filt_im * grad_im, filt_re * grad_im - filt_im * grad_re], axis=1))
                mixed_re, mixed_im = mixed_re * factor, mixed_im * factor
                products.append(jnp.concatenate([
                    mixed_re * grad_re + mixed_im * grad_im, mixed_re * grad_im - mixed_im * grad_re], axis=1))
        back = dot_parts(jnp.concatenate(products, axis=0), high[...], low[...], 1)
        inverted[begin:end] = back.reshape(end - begin, products_rows, 2 * LANES)

    for part in range(parts):
        def backward(tile, carry):
            start = pl.multiple_of(tile * 8, 8)
            at = pl.ds(pl.multiple_of(part * 3 * share + start, 8), 8)
            spec = {}
            for k1 in range(blocks + 1):
                re, im = inverted[k1, at, :LANES], inverted[k1, at, LANES:]
                cosine, sine = twiddles[k1, 0], twiddles[k1, 1]
                spec[k1] = (re * cosine - im * sine, re * sine + im * cosine)
            values = real_inverse(spec, rows_all, True)
            for x in range(lines):
                for z in range(columns):
                    result[source(x, part, z), pl.ds(start, 8), :] = values[x * columns + z]
            return carry

        lax.fori_loop(0, 3 * share // 8, backward, 0)


def unpack_kernel(seq_len, returned, gate_in, values_in, skip_gain, grad_out, gate_out,
                  grad_gate_out, grad_gate_in, grad_values, grad_filter):
    share = returned.shape[1] // 3
    for lane in range(0, gate_in.shape[1], LANES):
        at = slice(lane, lane + LANES)
        values, gate = values_in[:, at].astype(jnp.float32), gate_in[:, at].astype(jnp.float32)
        cotangent = grad_out[:, at].astype(jnp.float32)
        skip = skip_gain[:, at]

        def turned(s):
            return jnp.concatenate(
                [returned[lane // share + b, s * share:(s + 1) * share, :] for b in range(LANES // share)],
                axis=0).T

        mixer_state = turned(0) + skip * (gate * values)
        grad_gate_out[:, at] = (cotangent * mixer_state).astype(jnp.bfloat16)
        grad_mix = turned(1) + skip * (cotangent * gate_out[:, at].astype(jnp.float32))
        grad_gate_in[:, at] = (grad_mix * values).astype(jnp.bfloat16)
        grad_values[:, at] = (grad_mix * gate).astype(jnp.bfloat16)
        grad_filter[:, at] = turned(2) * (1.0 / math.sqrt(seq_len))


def pack(width, devices, parts, members, signals):
    operands = [factor for signal in members for factor in signals[signal]]
    tokens, channels = operands[0].shape
    share = channels // devices
    rows = sum(rows_of(signal, share, parts) for signal in members)
    return pl.pallas_call(
        lambda *refs: pack_kernel(share, parts, members, *refs),
        grid=(channels // width,),
        in_specs=[pl.BlockSpec((tokens, width), lambda i: (0, i))] * len(operands),
        out_specs=pl.BlockSpec((width // share, rows, tokens), lambda i: (i, 0, 0)),
        out_shape=jax.ShapeDtypeStruct((devices, rows, tokens), jnp.float32),
        compiler_params=pltpu.CompilerParams(vmem_limit_bytes=16 * 1024 * 1024),
        name="pack",
    )(*operands)


def convolve(shape, share, plan, received, constants):
    devices, _, tokens = received[0].shape
    blocks = shape[0] * shape[2]
    forward_rows = (2 * shape[1] + 1) * share
    inverse_rows = 3 * shape[1] * share
    return pl.pallas_call(
        lambda *refs: convolve_kernel(shape, plan, *refs),
        out_shape=jax.ShapeDtypeStruct((devices, 3 * share, tokens), jnp.float32),
        in_specs=[pl.BlockSpec(memory_space=pltpu.VMEM)] * (len(plan) + len(constants)),
        out_specs=pl.BlockSpec(memory_space=pltpu.VMEM),
        scratch_shapes=[pltpu.VMEM((blocks + 1, forward_rows, 2 * LANES), jnp.float32),
                        pltpu.VMEM((blocks + 1, inverse_rows, 2 * LANES), jnp.float32)],
        compiler_params=pltpu.CompilerParams(vmem_limit_bytes=24 * 1024 * 1024),
        name="convolve",
    )(*received, *constants)


def unpack(width, seq_len, returned, gate_in, values_in, skip_gain, grad_out, gate_out):
    devices, rows, tokens = returned.shape
    channels = gate_in.shape[1]
    share = channels // devices
    plain = pl.BlockSpec((tokens, width), lambda i: (0, i))
    wide = [jax.ShapeDtypeStruct((tokens, channels), jnp.bfloat16)] * 3
    return tuple(pl.pallas_call(
        lambda *refs: unpack_kernel(seq_len, *refs),
        grid=(channels // width,),
        in_specs=[pl.BlockSpec((width // share, rows, tokens), lambda i: (i, 0, 0)), plain, plain,
                  pl.BlockSpec((1, width), lambda i: (0, i)), plain, plain],
        out_specs=[plain] * 4,
        out_shape=wide + [jax.ShapeDtypeStruct((tokens, channels), jnp.float32)],
        compiler_params=pltpu.CompilerParams(vmem_limit_bytes=16 * 1024 * 1024),
        name="unpack",
    )(returned, gate_in, values_in, skip_gain[None, :], grad_out, gate_out))


GROUP = 3
PACK_WIDTH = 512
UNPACK_WIDTH = 512
MIXED, FILTER, GRAD = 0, 1, 2
FACTORS = (2, 1, 2)
WHOLE = ((MIXED, FILTER, GRAD),)
FILTER_FIRST = ((FILTER,), (MIXED, GRAD))


def local(gate_out, gate_in, values_in, long_filter, skip_gain, grad_out):
    tokens, channels = gate_out.shape
    shape = tuple(lax.axis_size(axis) for axis in AXES)
    devices = math.prod(shape)
    blocks = shape[0] * shape[2]
    constants = [jnp.asarray(t) for t in tables(blocks)]

    def exchange(operand):
        return lax.all_to_all(operand, AXES, split_axis=0, concat_axis=0, tiled=True)

    def there_and_back(plan):
        def run(gate_out, gate_in, values_in, long_filter, skip_gain, grad_out):
            signals = {MIXED: (gate_in, values_in), FILTER: (long_filter,), GRAD: (grad_out, gate_out)}
            received = []
            for members in plan:
                part = pack(PACK_WIDTH, devices, shape[1], members, signals)
                if received:
                    part, _ = lax.optimization_barrier((part, received[-1][0, 0, 0]))
                received.append(exchange(part))
            returned = exchange(convolve(shape, channels // devices, plan, received, constants))
            return unpack(UNPACK_WIDTH, tokens * blocks, returned, gate_in, values_in, skip_gain, grad_out, gate_out)
        return run

    return lax.cond(
        lax.axis_index("tensor") % 2 == 0, there_and_back(WHOLE), there_and_back(FILTER_FIRST),
        gate_out, gate_in, values_in, long_filter, skip_gain, grad_out)


def solution(mesh):
    parts, tensor, context = mesh.devices.shape
    lines = 2
    mesh = jax.sharding.Mesh(
        mesh.devices.reshape(parts, tensor, lines, context // lines), ("dp", "tensor", "line", "column"))
    sequence = P(("dp", "line", "column"), "tensor")
    return jax.shard_map(
        local,
        mesh=mesh,
        in_specs=(sequence, sequence, sequence, P(("line", "column"), "tensor"), P("tensor"), sequence),
        out_specs=(sequence,) * 4,
        check_vma=False,
    )
```

```python
import math

import jax
import jax.numpy as jnp
import numpy as np
from jax import lax
from jax.experimental import pallas as pl
from jax.experimental.pallas import tpu as pltpu
from jax.sharding import PartitionSpec as P

LANES = 128
AXES = ("line", "dp", "column")


def complex_add(a, b):
    return (a[0] + b[0], a[1] + b[1])


def complex_sub(a, b):
    return (a[0] - b[0], a[1] - b[1])


def rotate(a, angle_num, angle_den):
    num = angle_num % angle_den
    re, im = a
    if num == 0:
        return a
    if 4 * num == angle_den:
        return (-im, re)
    if 2 * num == angle_den:
        return (-re, -im)
    if 4 * num == 3 * angle_den:
        return (im, -re)
    if (8 * num) % angle_den == 0:
        half = math.sqrt(0.5)
        octant = (8 * num) // angle_den
        if octant == 1:
            return ((re - im) * half, (re + im) * half)
        if octant == 3:
            return ((re + im) * -half, (re - im) * half)
        if octant == 5:
            return ((im - re) * half, (re + im) * -half)
        return ((re + im) * half, (im - re) * half)
    c = math.cos(2.0 * math.pi * num / angle_den)
    s = math.sin(2.0 * math.pi * num / angle_den)
    return (re * c - im * s, re * s + im * c)


def complex_fft(values, sign):
    n = len(values)
    if n == 1:
        return values
    half = n // 2
    sums = [complex_add(values[p], values[p + half]) for p in range(half)]
    diffs = [complex_sub(values[p], values[p + half]) for p in range(half)]
    diffs = [rotate(d, sign * p, n) for p, d in enumerate(diffs)]
    even = complex_fft(sums, sign)
    odd = complex_fft(diffs, sign)
    return [v for pair in zip(even, odd) for v in pair]


def odd_forward(diffs, n, out):
    quarter = n // 4
    if n == 2:
        out[1] = (diffs[0], None)
        return
    twisted = [rotate((diffs[p], -diffs[p + quarter]), -p, n) for p in range(quarter)]
    for r, value in enumerate(complex_fft(twisted, -1)):
        k = 4 * r + 1
        if 2 * k < n:
            out[k] = value
        else:
            out[n - k] = (value[0], -value[1])


def real_forward(values, n):
    out = {}
    half = n // 2
    if len(values) == half:
        sums, diffs = values, values
    else:
        sums = [values[p] + values[p + half] for p in range(half)]
        diffs = [values[p] - values[p + half] for p in range(half)]
    if half == 1:
        out[0] = (sums[0], None)
    else:
        for k, value in real_forward(sums, half).items():
            out[2 * k] = value
    odd_forward(diffs, n, out)
    return out


def real_inverse(spec, n, first_half):
    half, quarter = n // 2, n // 4
    if n == 2:
        return [spec[0][0] + spec[1][0], spec[0][0] - spec[1][0]]
    evens = real_inverse({k // 2: v for k, v in spec.items() if k % 2 == 0}, half, False)
    odds = []
    for r in range(quarter):
        k = 4 * r + 1
        odds.append(spec[k] if 2 * k < n else (spec[n - k][0], -spec[n - k][1]))
    turned = [rotate(v, p, n) for p, v in enumerate(complex_fft(odds, 1))]
    odd_part = [v[0] for v in turned] + [-v[1] for v in turned]
    front = [evens[p] + odd_part[p] for p in range(half)]
    if first_half:
        return front
    return front + [evens[p] - odd_part[p] for p in range(half)]


def tables(blocks):
    rows_all = 2 * blocks
    lane = np.arange(LANES)
    angles = 2.0 * np.pi * (lane[:, None] * lane[None, :] % LANES) / LANES
    cosine, sine = np.cos(angles), np.sin(angles)
    whole = np.block([[cosine, -sine], [sine, cosine]]).astype(np.float32)
    high = whole.astype(jnp.bfloat16)
    low = (whole - high.astype(np.float32)).astype(jnp.bfloat16)
    turn = 2.0 * np.pi * np.arange(blocks + 1)[:, None] * lane[None, :] / (rows_all * LANES)
    twiddles = np.stack([np.cos(turn), np.sin(turn)], axis=1).astype(np.float32)
    return high, low, np.repeat(twiddles[:, :, None, :], 8, axis=2)


def split(value):
    high = value.astype(jnp.bfloat16)
    return high, (value - high.astype(jnp.float32)).astype(jnp.bfloat16)


def dot_parts(left, right_high, right_low, right_dim):
    dims = (((1,), (right_dim,)), ((), ()))
    high, low = split(left)
    total = lax.dot_general(low, right_high, dims, preferred_element_type=jnp.float32)
    total += lax.dot_general(high, right_low, dims, preferred_element_type=jnp.float32)
    return total + lax.dot_general(high, right_high, dims, preferred_element_type=jnp.float32)


def rows_of(signal, share, parts):
    return share // parts if signal == FILTER else share


def pack_kernel(share, parts, members, *refs):
    packed = refs[-1]
    part = lax.axis_index("dp")
    used = given = 0
    for signal in members:
        factors = refs[used:used + FACTORS[signal]]
        used += FACTORS[signal]
        count = rows_of(signal, share, parts)
        for lane in range(0, packed.shape[0] * share, LANES):
            value = factors[0][:, lane:lane + LANES].astype(jnp.float32)
            for factor in factors[1:]:
                value *= factor[:, lane:lane + LANES].astype(jnp.float32)
            turned = value.T
            for b in range(LANES // share):
                kept = turned[b * share:b * share + count]
                for other in range(1, share // count):
                    start = b * share + other * count
                    kept = jnp.where(part == other, turned[start:start + count], kept)
                packed[lane // share + b, given:given + count, :] = kept
        given += count


def convolve_kernel(shape, plan, *refs):
    received, (high, low, twiddles, result, spectrum, inverted) = refs[:len(plan)], refs[len(plan):]
    lines, parts, columns = shape
    blocks = lines * columns
    share = result.shape[1] // 3
    rows_all = 2 * blocks
    scale = 2.0 / (rows_all * LANES)
    grad_row, filt_row = parts * share, 2 * parts * share
    first_row = {MIXED: 0, GRAD: grad_row, FILTER: filt_row}

    def source(line, part, column):
        return (line * parts + part) * columns + column

    for operand, members in zip(received, plan):
        taken_row = 0
        for signal in members:
            count = rows_of(signal, share, parts)
            for part in range(parts):
                given_row = first_row[signal] + part * count

                def forward(tile, carry):
                    taken = pl.ds(pl.multiple_of(taken_row + tile * 8, 8), 8)
                    given = pl.ds(pl.multiple_of(given_row + tile * 8, 8), 8)
                    out = real_forward(
                        [operand[source(x, part, z), taken, :] for x in range(lines) for z in range(columns)],
                        rows_all)
                    for k1 in range(blocks + 1):
                        re, im = out[k1]
                        cosine, sine = twiddles[k1, 0], twiddles[k1, 1]
                        if im is None:
                            spectrum[k1, given, :LANES] = re * cosine
                            spectrum[k1, given, LANES:] = re * -sine
                        else:
                            spectrum[k1, given, :LANES] = re * cosine + im * sine
                            spectrum[k1, given, LANES:] = im * cosine - re * sine
                    return carry

                lax.fori_loop(0, count // 8, forward, 0, unroll=True)
            taken_row += count

    rows, products_rows = spectrum.shape[1], inverted.shape[1]
    for begin in range(0, blocks + 1, GROUP):
        end = min(begin + GROUP, blocks + 1)
        freqs = dot_parts(spectrum[begin:end].reshape((end - begin) * rows, 2 * LANES), high[...], low[...], 0)
        products = []
        for k1 in range(begin, end):
            freq = freqs[(k1 - begin) * rows:(k1 - begin + 1) * rows]
            factor = scale * 0.5 if k1 in (0, blocks) else scale
            filt_re, filt_im = freq[filt_row:, :LANES], freq[filt_row:, LANES:]
            filt_re, filt_im = filt_re * factor, filt_im * factor
            for part in range(parts):
                mixed = slice(part * share, (part + 1) * share)
                grad = slice(grad_row + part * share, grad_row + (part + 1) * share)
                mixed_re, mixed_im = freq[mixed, :LANES], freq[mixed, LANES:]
                grad_re, grad_im = freq[grad, :LANES], freq[grad, LANES:]
                products.append(jnp.concatenate([
                    filt_re * mixed_re - filt_im * mixed_im, filt_re * mixed_im + filt_im * mixed_re], axis=1))
                products.append(jnp.concatenate([
                    filt_re * grad_re + filt_im * grad_im, filt_re * grad_im - filt_im * grad_re], axis=1))
                mixed_re, mixed_im = mixed_re * factor, mixed_im * factor
                products.append(jnp.concatenate([
                    mixed_re * grad_re + mixed_im * grad_im, mixed_re * grad_im - mixed_im * grad_re], axis=1))
        back = dot_parts(jnp.concatenate(products, axis=0), high[...], low[...], 1)
        inverted[begin:end] = back.reshape(end - begin, products_rows, 2 * LANES)

    for part in range(parts):
        def backward(tile, carry):
            start = pl.multiple_of(tile * 8, 8)
            at = pl.ds(pl.multiple_of(part * 3 * share + start, 8), 8)
            spec = {}
            for k1 in range(blocks + 1):
                re, im = inverted[k1, at, :LANES], inverted[k1, at, LANES:]
                cosine, sine = twiddles[k1, 0], twiddles[k1, 1]
                spec[k1] = (re * cosine - im * sine, re * sine + im * cosine)
            values = real_inverse(spec, rows_all, True)
            for x in range(lines):
                for z in range(columns):
                    result[source(x, part, z), pl.ds(start, 8), :] = values[x * columns + z]
            return carry

        lax.fori_loop(0, 3 * share // 8, backward, 0, unroll=True)


def unpack_kernel(seq_len, returned, gate_in, values_in, skip_gain, grad_out, gate_out,
                  grad_gate_out, grad_gate_in, grad_values, grad_filter):
    share = returned.shape[1] // 3
    for lane in range(0, gate_in.shape[1], LANES):
        at = slice(lane, lane + LANES)
        values, gate = values_in[:, at].astype(jnp.float32), gate_in[:, at].astype(jnp.float32)
        cotangent = grad_out[:, at].astype(jnp.float32)
        skip = skip_gain[:, at]

        def turned(s):
            return jnp.concatenate(
                [returned[lane // share + b, s * share:(s + 1) * share, :] for b in range(LANES // share)],
                axis=0).T

        mixer_state = turned(0) + skip * (gate * values)
        grad_gate_out[:, at] = (cotangent * mixer_state).astype(jnp.bfloat16)
        grad_mix = turned(1) + skip * (cotangent * gate_out[:, at].astype(jnp.float32))
        grad_gate_in[:, at] = (grad_mix * values).astype(jnp.bfloat16)
        grad_values[:, at] = (grad_mix * gate).astype(jnp.bfloat16)
        grad_filter[:, at] = turned(2) * (1.0 / math.sqrt(seq_len))


def pack(width, devices, parts, members, signals):
    operands = [factor for signal in members for factor in signals[signal]]
    tokens, channels = operands[0].shape
    share = channels // devices
    rows = sum(rows_of(signal, share, parts) for signal in members)
    return pl.pallas_call(
        lambda *refs: pack_kernel(share, parts, members, *refs),
        grid=(channels // width,),
        in_specs=[pl.BlockSpec((tokens, width), lambda i: (0, i))] * len(operands),
        out_specs=pl.BlockSpec((width // share, rows, tokens), lambda i: (i, 0, 0)),
        out_shape=jax.ShapeDtypeStruct((devices, rows, tokens), jnp.float32),
        compiler_params=pltpu.CompilerParams(vmem_limit_bytes=16 * 1024 * 1024),
        name="pack",
    )(*operands)


def convolve(shape, share, plan, received, constants):
    devices, _, tokens = received[0].shape
    blocks = shape[0] * shape[2]
    forward_rows = (2 * shape[1] + 1) * share
    inverse_rows = 3 * shape[1] * share
    return pl.pallas_call(
        lambda *refs: convolve_kernel(shape, plan, *refs),
        out_shape=jax.ShapeDtypeStruct((devices, 3 * share, tokens), jnp.float32),
        in_specs=[pl.BlockSpec(memory_space=pltpu.VMEM)] * (len(plan) + len(constants)),
        out_specs=pl.BlockSpec(memory_space=pltpu.VMEM),
        scratch_shapes=[pltpu.VMEM((blocks + 1, forward_rows, 2 * LANES), jnp.float32),
                        pltpu.VMEM((blocks + 1, inverse_rows, 2 * LANES), jnp.float32)],
        compiler_params=pltpu.CompilerParams(vmem_limit_bytes=24 * 1024 * 1024),
        name="convolve",
    )(*received, *constants)


def unpack(width, seq_len, returned, gate_in, values_in, skip_gain, grad_out, gate_out):
    devices, rows, tokens = returned.shape
    channels = gate_in.shape[1]
    share = channels // devices
    plain = pl.BlockSpec((tokens, width), lambda i: (0, i))
    wide = [jax.ShapeDtypeStruct((tokens, channels), jnp.bfloat16)] * 3
    return tuple(pl.pallas_call(
        lambda *refs: unpack_kernel(seq_len, *refs),
        grid=(channels // width,),
        in_specs=[pl.BlockSpec((width // share, rows, tokens), lambda i: (i, 0, 0)), plain, plain,
                  pl.BlockSpec((1, width), lambda i: (0, i)), plain, plain],
        out_specs=[plain] * 4,
        out_shape=wide + [jax.ShapeDtypeStruct((tokens, channels), jnp.float32)],
        compiler_params=pltpu.CompilerParams(vmem_limit_bytes=16 * 1024 * 1024),
        name="unpack",
    )(returned, gate_in, values_in, skip_gain[None, :], grad_out, gate_out))


GROUP = 3
PACK_WIDTH = 512
UNPACK_WIDTH = 512
MIXED, FILTER, GRAD = 0, 1, 2
FACTORS = (2, 1, 2)
WHOLE = ((MIXED, FILTER, GRAD),)
FILTER_FIRST = ((FILTER,), (MIXED, GRAD))


def local(gate_out, gate_in, values_in, long_filter, skip_gain, grad_out):
    tokens, channels = gate_out.shape
    shape = tuple(lax.axis_size(axis) for axis in AXES)
    devices = math.prod(shape)
    blocks = shape[0] * shape[2]
    constants = [jnp.asarray(t) for t in tables(blocks)]

    def exchange(operand):
        return lax.all_to_all(operand, AXES, split_axis=0, concat_axis=0, tiled=True)

    def there_and_back(plan):
        def run(gate_out, gate_in, values_in, long_filter, skip_gain, grad_out):
            signals = {MIXED: (gate_in, values_in), FILTER: (long_filter,), GRAD: (grad_out, gate_out)}
            received = []
            for members in plan:
                part = pack(PACK_WIDTH, devices, shape[1], members, signals)
                if received:
                    part, _ = lax.optimization_barrier((part, received[-1][0, 0, 0]))
                received.append(exchange(part))
            returned = exchange(convolve(shape, channels // devices, plan, received, constants))
            return unpack(UNPACK_WIDTH, tokens * blocks, returned, gate_in, values_in, skip_gain, grad_out, gate_out)
        return run

    return lax.cond(
        lax.axis_index("tensor") % 2 == 0, there_and_back(WHOLE), there_and_back(FILTER_FIRST),
        gate_out, gate_in, values_in, long_filter, skip_gain, grad_out)


def solution(mesh):
    parts, tensor, context = mesh.devices.shape
    lines = 2
    mesh = jax.sharding.Mesh(
        mesh.devices.reshape(parts, tensor, lines, context // lines), ("dp", "tensor", "line", "column"))
    sequence = P(("dp", "line", "column"), "tensor")
    return jax.shard_map(
        local,
        mesh=mesh,
        in_specs=(sequence, sequence, sequence, P(("line", "column"), "tensor"), P("tensor"), sequence),
        out_specs=(sequence,) * 4,
        check_vma=False,
    )
```

```python
import math

import jax
import jax.numpy as jnp
import numpy as np
from jax import lax
from jax.experimental import pallas as pl
from jax.experimental.pallas import tpu as pltpu
from jax.sharding import PartitionSpec as P

LANES = 128
AXES = ("line", "dp", "column")


def complex_add(a, b):
    return (a[0] + b[0], a[1] + b[1])


def complex_sub(a, b):
    return (a[0] - b[0], a[1] - b[1])


def rotate(a, angle_num, angle_den):
    num = angle_num % angle_den
    re, im = a
    if num == 0:
        return a
    if 4 * num == angle_den:
        return (-im, re)
    if 2 * num == angle_den:
        return (-re, -im)
    if 4 * num == 3 * angle_den:
        return (im, -re)
    if (8 * num) % angle_den == 0:
        half = math.sqrt(0.5)
        octant = (8 * num) // angle_den
        if octant == 1:
            return ((re - im) * half, (re + im) * half)
        if octant == 3:
            return ((re + im) * -half, (re - im) * half)
        if octant == 5:
            return ((im - re) * half, (re + im) * -half)
        return ((re + im) * half, (im - re) * half)
    c = math.cos(2.0 * math.pi * num / angle_den)
    s = math.sin(2.0 * math.pi * num / angle_den)
    return (re * c - im * s, re * s + im * c)


def complex_fft(values, sign):
    n = len(values)
    if n == 1:
        return values
    half = n // 2
    sums = [complex_add(values[p], values[p + half]) for p in range(half)]
    diffs = [complex_sub(values[p], values[p + half]) for p in range(half)]
    diffs = [rotate(d, sign * p, n) for p, d in enumerate(diffs)]
    even = complex_fft(sums, sign)
    odd = complex_fft(diffs, sign)
    return [v for pair in zip(even, odd) for v in pair]


def odd_forward(diffs, n, out):
    quarter = n // 4
    if n == 2:
        out[1] = (diffs[0], None)
        return
    twisted = [rotate((diffs[p], -diffs[p + quarter]), -p, n) for p in range(quarter)]
    for r, value in enumerate(complex_fft(twisted, -1)):
        k = 4 * r + 1
        if 2 * k < n:
            out[k] = value
        else:
            out[n - k] = (value[0], -value[1])


def real_forward(values, n):
    out = {}
    half = n // 2
    if len(values) == half:
        sums, diffs = values, values
    else:
        sums = [values[p] + values[p + half] for p in range(half)]
        diffs = [values[p] - values[p + half] for p in range(half)]
    if half == 1:
        out[0] = (sums[0], None)
    else:
        for k, value in real_forward(sums, half).items():
            out[2 * k] = value
    odd_forward(diffs, n, out)
    return out


def real_inverse(spec, n, first_half):
    half, quarter = n // 2, n // 4
    if n == 2:
        return [spec[0][0] + spec[1][0], spec[0][0] - spec[1][0]]
    evens = real_inverse({k // 2: v for k, v in spec.items() if k % 2 == 0}, half, False)
    odds = []
    for r in range(quarter):
        k = 4 * r + 1
        odds.append(spec[k] if 2 * k < n else (spec[n - k][0], -spec[n - k][1]))
    turned = [rotate(v, p, n) for p, v in enumerate(complex_fft(odds, 1))]
    odd_part = [v[0] for v in turned] + [-v[1] for v in turned]
    front = [evens[p] + odd_part[p] for p in range(half)]
    if first_half:
        return front
    return front + [evens[p] - odd_part[p] for p in range(half)]


def tables(blocks):
    rows_all = 2 * blocks
    lane = np.arange(LANES)
    angles = 2.0 * np.pi * (lane[:, None] * lane[None, :] % LANES) / LANES
    cosine, sine = np.cos(angles), np.sin(angles)
    whole = np.block([[cosine, -sine], [sine, cosine]]).astype(np.float32)
    high = whole.astype(jnp.bfloat16)
    low = (whole - high.astype(np.float32)).astype(jnp.bfloat16)
    turn = 2.0 * np.pi * np.arange(blocks + 1)[:, None] * lane[None, :] / (rows_all * LANES)
    twiddles = np.stack([np.cos(turn), np.sin(turn)], axis=1).astype(np.float32)
    return high, low, np.repeat(twiddles[:, :, None, :], 8, axis=2)


def split(value):
    high = value.astype(jnp.bfloat16)
    return high, (value - high.astype(jnp.float32)).astype(jnp.bfloat16)


def dot_parts(left, right_high, right_low, right_dim):
    dims = (((1,), (right_dim,)), ((), ()))
    high, low = split(left)
    total = lax.dot_general(low, right_high, dims, preferred_element_type=jnp.float32)
    total += lax.dot_general(high, right_low, dims, preferred_element_type=jnp.float32)
    return total + lax.dot_general(high, right_high, dims, preferred_element_type=jnp.float32)


def rows_of(signal, share, parts):
    return share // parts if signal == FILTER else share


def pack_kernel(share, parts, members, *refs):
    packed = refs[-1]
    part = lax.axis_index("dp")
    used = given = 0
    for signal in members:
        factors = refs[used:used + FACTORS[signal]]
        used += FACTORS[signal]
        count = rows_of(signal, share, parts)
        for lane in range(0, packed.shape[0] * share, LANES):
            value = factors[0][:, lane:lane + LANES].astype(jnp.float32)
            for factor in factors[1:]:
                value *= factor[:, lane:lane + LANES].astype(jnp.float32)
            turned = value.T
            for b in range(LANES // share):
                kept = turned[b * share:b * share + count]
                for other in range(1, share // count):
                    start = b * share + other * count
                    kept = jnp.where(part == other, turned[start:start + count], kept)
                packed[lane // share + b, given:given + count, :] = kept
        given += count


def convolve_kernel(shape, plan, *refs):
    received, (high, low, twiddles, result, spectrum, inverted) = refs[:len(plan)], refs[len(plan):]
    lines, parts, columns = shape
    blocks = lines * columns
    share = result.shape[1] // 3
    rows_all = 2 * blocks
    scale = 2.0 / (rows_all * LANES)
    grad_row, filt_row = parts * share, 2 * parts * share
    first_row = {MIXED: 0, GRAD: grad_row, FILTER: filt_row}

    def source(line, part, column):
        return (line * parts + part) * columns + column

    for operand, members in zip(received, plan):
        taken_row = 0
        for signal in members:
            count = rows_of(signal, share, parts)
            for part in range(parts):
                given_row = first_row[signal] + part * count

                def forward(tile, carry):
                    taken = pl.ds(pl.multiple_of(taken_row + tile * 8, 8), 8)
                    given = pl.ds(pl.multiple_of(given_row + tile * 8, 8), 8)
                    out = real_forward(
                        [operand[source(x, part, z), taken, :] for x in range(lines) for z in range(columns)],
                        rows_all)
                    for k1 in range(blocks + 1):
                        re, im = out[k1]
                        cosine, sine = twiddles[k1, 0], twiddles[k1, 1]
                        if im is None:
                            spectrum[k1, given, :LANES] = re * cosine
                            spectrum[k1, given, LANES:] = re * -sine
                        else:
                            spectrum[k1, given, :LANES] = re * cosine + im * sine
                            spectrum[k1, given, LANES:] = im * cosine - re * sine
                    return carry

                lax.fori_loop(0, count // 8, forward, 0, unroll=True)
            taken_row += count

    rows, products_rows = spectrum.shape[1], inverted.shape[1]
    for begin in range(0, blocks + 1, GROUP):
        end = min(begin + GROUP, blocks + 1)
        freqs = dot_parts(spectrum[begin:end].reshape((end - begin) * rows, 2 * LANES), high[...], low[...], 0)
        products = []
        for k1 in range(begin, end):
            freq = freqs[(k1 - begin) * rows:(k1 - begin + 1) * rows]
            factor = scale * 0.5 if k1 in (0, blocks) else scale
            filt_re, filt_im = freq[filt_row:, :LANES], freq[filt_row:, LANES:]
            filt_re, filt_im = filt_re * factor, filt_im * factor
            for part in range(parts):
                mixed = slice(part * share, (part + 1) * share)
                grad = slice(grad_row + part * share, grad_row + (part + 1) * share)
                mixed_re, mixed_im = freq[mixed, :LANES], freq[mixed, LANES:]
                grad_re, grad_im = freq[grad, :LANES], freq[grad, LANES:]
                products.append(jnp.concatenate([
                    filt_re * mixed_re - filt_im * mixed_im, filt_re * mixed_im + filt_im * mixed_re], axis=1))
                products.append(jnp.concatenate([
                    filt_re * grad_re + filt_im * grad_im, filt_re * grad_im - filt_im * grad_re], axis=1))
                mixed_re, mixed_im = mixed_re * factor, mixed_im * factor
                products.append(jnp.concatenate([
                    mixed_re * grad_re + mixed_im * grad_im, mixed_re * grad_im - mixed_im * grad_re], axis=1))
        back = dot_parts(jnp.concatenate(products, axis=0), high[...], low[...], 1)
        inverted[begin:end] = back.reshape(end - begin, products_rows, 2 * LANES)

    for part in range(parts):
        def backward(tile, carry):
            start = pl.multiple_of(tile * 8, 8)
            at = pl.ds(pl.multiple_of(part * 3 * share + start, 8), 8)
            spec = {}
            for k1 in range(blocks + 1):
                re, im = inverted[k1, at, :LANES], inverted[k1, at, LANES:]
                cosine, sine = twiddles[k1, 0], twiddles[k1, 1]
                spec[k1] = (re * cosine - im * sine, re * sine + im * cosine)
            values = real_inverse(spec, rows_all, True)
            for x in range(lines):
                for z in range(columns):
                    result[source(x, part, z), pl.ds(start, 8), :] = values[x * columns + z]
            return carry

        lax.fori_loop(0, 3 * share // 8, backward, 0, unroll=True)


def unpack_kernel(seq_len, returned, gate_in, values_in, skip_gain, grad_out, gate_out,
                  grad_gate_out, grad_gate_in, grad_values, grad_filter):
    share = returned.shape[1] // 3
    for lane in range(0, gate_in.shape[1], LANES):
        at = slice(lane, lane + LANES)
        values, gate = values_in[:, at].astype(jnp.float32), gate_in[:, at].astype(jnp.float32)
        cotangent = grad_out[:, at].astype(jnp.float32)
        skip = skip_gain[:, at]

        def turned(s):
            return jnp.concatenate(
                [returned[lane // share + b, s * share:(s + 1) * share, :] for b in range(LANES // share)],
                axis=0).T

        mixer_state = turned(0) + skip * (gate * values)
        grad_gate_out[:, at] = (cotangent * mixer_state).astype(jnp.bfloat16)
        grad_mix = turned(1) + skip * (cotangent * gate_out[:, at].astype(jnp.float32))
        grad_gate_in[:, at] = (grad_mix * values).astype(jnp.bfloat16)
        grad_values[:, at] = (grad_mix * gate).astype(jnp.bfloat16)
        grad_filter[:, at] = turned(2) * (1.0 / math.sqrt(seq_len))


def pack(width, devices, parts, members, signals):
    operands = [factor for signal in members for factor in signals[signal]]
    tokens, channels = operands[0].shape
    share = channels // devices
    rows = sum(rows_of(signal, share, parts) for signal in members)
    return pl.pallas_call(
        lambda *refs: pack_kernel(share, parts, members, *refs),
        grid=(channels // width,),
        in_specs=[pl.BlockSpec((tokens, width), lambda i: (0, i))] * len(operands),
        out_specs=pl.BlockSpec((width // share, rows, tokens), lambda i: (i, 0, 0)),
        out_shape=jax.ShapeDtypeStruct((devices, rows, tokens), jnp.float32),
        compiler_params=pltpu.CompilerParams(vmem_limit_bytes=16 * 1024 * 1024),
        name="pack",
    )(*operands)


def convolve(shape, share, plan, received, constants):
    devices, _, tokens = received[0].shape
    blocks = shape[0] * shape[2]
    forward_rows = (2 * shape[1] + 1) * share
    inverse_rows = 3 * shape[1] * share
    return pl.pallas_call(
        lambda *refs: convolve_kernel(shape, plan, *refs),
        out_shape=jax.ShapeDtypeStruct((devices, 3 * share, tokens), jnp.float32),
        in_specs=[pl.BlockSpec(memory_space=pltpu.VMEM)] * (len(plan) + len(constants)),
        out_specs=pl.BlockSpec(memory_space=pltpu.VMEM),
        scratch_shapes=[pltpu.VMEM((blocks + 1, forward_rows, 2 * LANES), jnp.float32),
                        pltpu.VMEM((blocks + 1, inverse_rows, 2 * LANES), jnp.float32)],
        compiler_params=pltpu.CompilerParams(vmem_limit_bytes=24 * 1024 * 1024),
        name="convolve",
    )(*received, *constants)


def unpack(width, seq_len, returned, gate_in, values_in, skip_gain, grad_out, gate_out):
    devices, rows, tokens = returned.shape
    channels = gate_in.shape[1]
    share = channels // devices
    plain = pl.BlockSpec((tokens, width), lambda i: (0, i))
    wide = [jax.ShapeDtypeStruct((tokens, channels), jnp.bfloat16)] * 3
    return tuple(pl.pallas_call(
        lambda *refs: unpack_kernel(seq_len, *refs),
        grid=(channels // width,),
        in_specs=[pl.BlockSpec((width // share, rows, tokens), lambda i: (i, 0, 0)), plain, plain,
                  pl.BlockSpec((1, width), lambda i: (0, i)), plain, plain],
        out_specs=[plain] * 4,
        out_shape=wide + [jax.ShapeDtypeStruct((tokens, channels), jnp.float32)],
        compiler_params=pltpu.CompilerParams(vmem_limit_bytes=16 * 1024 * 1024),
        name="unpack",
    )(returned, gate_in, values_in, skip_gain[None, :], grad_out, gate_out))


GROUP = 3
PACK_WIDTH = 512
UNPACK_WIDTH = 1024
MIXED, FILTER, GRAD = 0, 1, 2
FACTORS = (2, 1, 2)
WHOLE = ((MIXED, FILTER, GRAD),)
FILTER_FIRST = ((FILTER,), (MIXED, GRAD))


def local(gate_out, gate_in, values_in, long_filter, skip_gain, grad_out):
    tokens, channels = gate_out.shape
    shape = tuple(lax.axis_size(axis) for axis in AXES)
    devices = math.prod(shape)
    blocks = shape[0] * shape[2]
    constants = [jnp.asarray(t) for t in tables(blocks)]

    def exchange(operand):
        return lax.all_to_all(operand, AXES, split_axis=0, concat_axis=0, tiled=True)

    def there_and_back(plan):
        def run(gate_out, gate_in, values_in, long_filter, skip_gain, grad_out):
            signals = {MIXED: (gate_in, values_in), FILTER: (long_filter,), GRAD: (grad_out, gate_out)}
            received = []
            for members in plan:
                part = pack(PACK_WIDTH, devices, shape[1], members, signals)
                if received:
                    part, _ = lax.optimization_barrier((part, received[-1][0, 0, 0]))
                received.append(exchange(part))
            returned = exchange(convolve(shape, channels // devices, plan, received, constants))
            return unpack(UNPACK_WIDTH, tokens * blocks, returned, gate_in, values_in, skip_gain, grad_out, gate_out)
        return run

    return lax.cond(
        lax.axis_index("tensor") % 2 == 0, there_and_back(WHOLE), there_and_back(FILTER_FIRST),
        gate_out, gate_in, values_in, long_filter, skip_gain, grad_out)


def solution(mesh):
    parts, tensor, context = mesh.devices.shape
    lines = 2
    mesh = jax.sharding.Mesh(
        mesh.devices.reshape(parts, tensor, lines, context // lines), ("dp", "tensor", "line", "column"))
    sequence = P(("dp", "line", "column"), "tensor")
    return jax.shard_map(
        local,
        mesh=mesh,
        in_specs=(sequence, sequence, sequence, P(("line", "column"), "tensor"), P("tensor"), sequence),
        out_specs=(sequence,) * 4,
        check_vma=False,
    )
```
